128 devices in a mesh: rows: 32 (over z, y, core), cols: 4 (over x).
Axes of the slice: x: 4, y: 4, z: 4, core: 2. Of those that a mesh axis runs over, the one named last changes fastest.
Arguments:
- activations: bfloat16 [8192, 65536], P('rows', 'cols'), as said below
- weight_tiles: bfloat16 [4, 64, 8, 128, 128], P('cols', 'rows'), may hold values from -0.1875 to 0.1875
- panel_map: int32 [4, 64], P('cols'), may hold values from 0 to 63, each once within a row
- block_index: int32 [256, 8], replicated, may hold values from 0 to 511, all different within a row
- active_list: int32 [32, 16], P('rows'), may hold values from 0 to 16, as said below
- bias: float32 [32768], P('cols'), may hold values from -1 to 0.5
Outputs:
- output: bfloat16 [8192, 32768], P('rows', 'cols')
The draws below stay inside these ranges and needn't reach their ends.
Inputs may be any that keep to these rules, and one draw needn't show every extreme that they name: Each row of panel_map holds every number of its range once. `block_index`: each output block column names 8 different input blocks; every input block is named by some column. `active_list`: each row group lists 16 // 2 to 16 different active row blocks below 16 in its first slots, in no particular order; its remaining slots hold 16. At least one row group has 16 active row blocks. `activations`: entries are zero or positive; row scales differ widely from sample to sample.
All inputs are finite; a program needn't handle non-finite values.
Results may differ from the reference program's by a relative error of at most 0.001.
Values may be sent and summed in bfloat16 or wider, within the bound.
A program may use at most 256 MiB of HBM per device.

```python
import math
import jax
import jax.numpy as jnp
from jax import lax

NEURONS = 65536
OUT_WINDOW = 32768
TILE = 128
K = 8
ROW_BLOCK = 16
BLOCKS_DEV = 16
ACT_MOST = 16
IN_BLOCKS = 512
OUT_BLOCKS = 256
PANELS = 64
ROW_GROUPS = 32
COL_GROUPS = 4
ROWS = 8192


def draw_activations(key, part):
    key = jax.random.fold_in(key, 7)
    scale_key, value_key = jax.random.split(key)
    scales = jnp.exp(jax.random.uniform(scale_key, (ROWS, 1), jnp.float32, math.log(0.3), math.log(60.0)))
    values = jnp.maximum(jax.random.normal(value_key, (ROWS, NEURONS), jnp.float32), 0.0)
    return (values * scales).astype(jnp.bfloat16)


def draw_active_list(key, part):
    key = jax.random.fold_in(key, 1)
    group_keys = jax.random.split(jax.random.fold_in(key, 5), ROW_GROUPS)
    orders = jax.vmap(lambda one_key: jax.random.permutation(one_key, BLOCKS_DEV))(group_keys)[:, :ACT_MOST]
    counts = jax.random.randint(jax.random.fold_in(key, 2), (ROW_GROUPS,), ACT_MOST // 2, ACT_MOST + 1)
    fullest = jax.random.randint(jax.random.fold_in(key, 3), (), 0, ROW_GROUPS)
    counts = jnp.where(jnp.arange(ROW_GROUPS) == fullest, ACT_MOST, counts)
    places = jnp.arange(ACT_MOST)
    return jnp.where(places[None, :] < counts[:, None], orders, BLOCKS_DEV).astype(jnp.int32)


def block_levels(own_key, shape, cuts, smallest, high):
    level, own = 1.0, jax.random.fold_in(own_key, 6)
    for axis_at, blocks in cuts:
        draws = jnp.exp(jax.random.uniform(jax.random.fold_in(own, axis_at), (blocks,), jnp.float32, smallest / len(cuts), high / len(cuts)))
        level = level * jnp.repeat(draws, shape[axis_at] // blocks).reshape([-1 if axis == axis_at else 1 for axis in range(len(shape))])
    return level


def distinct(rng, rows, count, top, lift):
    ranking = jax.random.permutation(jax.random.fold_in(rng, 1), count)
    boost = ranking
    for power in range(3):
        boost = boost * boost // count
    boost = boost * lift // count
    chance = jax.random.randint(jax.random.fold_in(rng, 2), (rows, count), 0, 4096) + boost
    sure = jax.random.permutation(jax.random.fold_in(rng, 3), rows)[jnp.arange(count) % rows]
    chance = jnp.where(jnp.arange(rows)[:, None] == sure[None, :], 1 << 14, chance)
    merit = chance * count + jnp.arange(count)
    return lax.top_k(merit.astype(jnp.int32), top)[1].astype(jnp.int32)


def gaussian(rng, extent, scale, most, cuts=(), kind=jnp.bfloat16):
    array = jax.random.normal(rng, extent, jnp.float32) * scale
    if len(cuts) > 0:
        array = block_levels(rng, extent, cuts, -0.22, 0.18) * array
    return jnp.clip(array, min=-most, max=most).astype(kind)


def setup_inputs(seed: int = 0) -> dict:
    key_list = jax.random.split(jax.random.key(seed), 7)
    activations = draw_activations(jax.random.fold_in(key_list[6], 71), 0)
    weight_tiles = gaussian(key_list[1], (COL_GROUPS, PANELS, K, TILE, TILE), (K * TILE) ** -0.5, 0.1875, ((0, 4), (1, 32)))
    panel_map = jax.vmap(lambda own: jax.random.permutation(own, PANELS))(jax.random.split(key_list[2], COL_GROUPS)).reshape((COL_GROUPS, PANELS)).astype(jnp.int32)
    block_index = distinct(key_list[3], OUT_BLOCKS, IN_BLOCKS, K, 0)
    active_list = draw_active_list(jax.random.fold_in(key_list[6], 71), 0)
    bias = jnp.clip(-1.0 + 1.5 * jax.random.uniform(key_list[5], (OUT_WINDOW,), jnp.float32) ** block_levels(key_list[5], (OUT_WINDOW,), ((0, 4),), -0.2, 0.2), -1.0, 0.5)
    return dict(activations=activations, weight_tiles=weight_tiles, panel_map=panel_map, block_index=block_index, active_list=active_list, bias=bias)


def reference(activations, weight_tiles, panel_map, block_index, active_list, bias):
    grouped = activations.reshape(ROW_GROUPS, BLOCKS_DEV, ROW_BLOCK, NEURONS)
    picked = jnp.minimum(active_list, BLOCKS_DEV - 1).astype(jnp.int32)
    compact = jax.vmap(lambda group_rows, group_pick: jnp.take(group_rows, group_pick, axis=0))(grouped, picked)
    slot_rows = ROW_GROUPS * ACT_MOST * ROW_BLOCK
    tile_view = compact.reshape(slot_rows, IN_BLOCKS, TILE)
    columns = (jnp.arange(COL_GROUPS, dtype=jnp.int32)[:, None] * PANELS + panel_map.astype(jnp.int32)).reshape(-1)
    sources = jnp.take(block_index, columns, axis=0).astype(jnp.int32)
    flat_tiles = weight_tiles.reshape(COL_GROUPS * PANELS, K, TILE, TILE)

    def one_panel(pair):
        inputs, panel_block = pair
        chosen = jnp.take(tile_view, inputs, axis=1).astype(jnp.float32)
        return jnp.einsum("mkt,kts->ms", chosen, panel_block.astype(jnp.float32))

    stored = lax.map(one_panel, (sources, flat_tiles))
    stored = stored.reshape(COL_GROUPS, PANELS, slot_rows, TILE)
    inverse = jnp.argsort(panel_map, axis=1)
    ordered = jax.vmap(lambda group_out, group_inv: jnp.take(group_out, group_inv, axis=0))(stored, inverse)
    ordered = jnp.transpose(ordered, (2, 0, 1, 3)).reshape(slot_rows, OUT_WINDOW)
    clamped = jnp.minimum(jnp.maximum(ordered + bias[None, :], 0.0), 32.0).astype(jnp.bfloat16)
    placing = (active_list[:, :, None] == jnp.arange(BLOCKS_DEV, dtype=jnp.int32)[None, None, :]).astype(jnp.float32)
    spread = jnp.einsum("gab,garw->gbrw", placing, clamped.reshape(ROW_GROUPS, ACT_MOST, ROW_BLOCK, OUT_WINDOW).astype(jnp.float32))
    return spread.astype(jnp.bfloat16).reshape(ROWS, OUT_WINDOW)
```

```python
import functools

import jax
import jax.numpy as jnp
from jax import lax
from jax.experimental import pallas as pl
from jax.experimental.pallas import tpu as pltpu
from jax.sharding import PartitionSpec as P

TILE = 128
ROW_BLOCK = 16
GROUPS = 4
PANELS = 64
DEPTH = 8
HERE = 128
LISTED = 98
PASSED = 48
OWN, LEFT = 0, HERE
RIGHT = LEFT + LISTED
FAR_LEFT = RIGHT + LISTED
FAR_RIGHT = FAR_LEFT + PASSED
SLOTS = FAR_RIGHT + PASSED
MESH = pl.DeviceIdType.MESH


def plan_kernel(place_ref, index_ref, map_ref, lists_ref, table_ref):
    place = place_ref[0]
    blocks = GROUPS * HERE
    lane = lax.broadcasted_iota(jnp.int32, (GROUPS * PANELS, blocks), 1)
    named = jnp.zeros((GROUPS * PANELS, blocks), jnp.float32)
    for k in range(DEPTH):
        named = jnp.where(index_ref[:, k : k + 1] == lane, 1.0, named)
    need = [jnp.max(named[c * PANELS : (c + 1) * PANELS], axis=0, keepdims=True) for c in range(GROUPS)]

    def asked(distance):
        return jnp.concatenate(
            [need[(s + distance) % GROUPS][:, s * HERE : (s + 1) * HERE] for s in range(GROUPS)], axis=0
        )

    right, far, left = asked(1), asked(2), asked(3)
    row = lax.broadcasted_iota(jnp.int32, (HERE, HERE), 0)
    col = lax.broadcasted_iota(jnp.int32, (HERE, HERE), 1)
    before = (row < col).astype(jnp.bfloat16)

    def rank(flags):
        return jnp.dot(flags.astype(jnp.bfloat16), before, preferred_element_type=jnp.float32)

    def count(flags):
        return jnp.sum(flags, axis=1, keepdims=True)

    both = far * right * left
    none = far * (1.0 - right) * (1.0 - left)
    only_right = far * right * (1.0 - left)
    only_left = far * left * (1.0 - right)
    none_n, both_n = count(none), count(both)
    cut = jnp.clip(jnp.floor((count(left) - count(right) + none_n) * 0.5), 0.0, none_n)
    tilt = count(only_left) + none_n - cut - count(only_right) - cut
    share = jnp.clip(jnp.floor((tilt + both_n) * 0.5), 0.0, both_n)
    by_right = only_right + none * (rank(none) < cut) + both * (rank(both) < share)
    by_left = far - by_right

    def order(passed, wanted):
        rest = wanted * (1.0 - passed)
        at = jnp.where(passed > 0.0, rank(passed), count(passed) + rank(rest))
        inside = passed + rest
        return jnp.where(inside > 0.0, at, -1.0), count(passed), count(inside)

    at_right, passed_right, listed_right = order(by_right, right)
    at_left, passed_left, listed_left = order(by_left, left)
    passed_most = jnp.max(jnp.maximum(passed_right, passed_left), axis=0, keepdims=True)
    listed_most = jnp.max(jnp.maximum(listed_right, listed_left), axis=0, keepdims=True)

    source = lax.broadcasted_iota(jnp.int32, (GROUPS, HERE), 0)
    mine = source == place
    slot = lax.broadcasted_iota(jnp.int32, (HERE, HERE), 0).astype(jnp.float32)
    ids = lax.broadcasted_iota(jnp.int32, (8, HERE), 1).astype(jnp.bfloat16)

    def listing(at):
        own = jnp.sum(jnp.where(mine, at, 0.0), axis=0, keepdims=True)
        hot = (own == slot).astype(jnp.bfloat16)
        out = lax.dot_general(ids, hot, (((1,), (1,)), ((), ())), preferred_element_type=jnp.float32)
        return out[:1]

    lists_ref[...] = jnp.concatenate(
        [
            listing(at_right),
            listing(at_left),
            jnp.broadcast_to(passed_most, (1, HERE)),
            jnp.broadcast_to(listed_most, (1, HERE)),
            jnp.zeros((4, HERE), jnp.float32),
        ],
        axis=0,
    ).astype(jnp.int32)

    ids_here = lax.broadcasted_iota(jnp.int32, (GROUPS, HERE), 1).astype(jnp.float32)
    from_left = LEFT + at_right
    from_right = RIGHT + at_left
    from_far = jnp.where(by_right > 0.0, FAR_LEFT + at_right, FAR_RIGHT + at_left)
    away = lax.rem(source - place + GROUPS, GROUPS)
    slots = jnp.where(
        away == 0,
        OWN + ids_here,
        jnp.where(away == 1, from_right, jnp.where(away == 2, from_far, from_left)),
    )
    slots = jnp.concatenate([slots[s : s + 1] for s in range(GROUPS)], axis=1)
    mine_index = index_ref[pl.ds(pl.multiple_of(place * PANELS, PANELS), PANELS), :]
    lane = lax.broadcasted_iota(jnp.int32, (PANELS, blocks), 1)
    columns = []
    for k in range(DEPTH):
        hit = mine_index[:, k : k + 1] == lane
        columns.append(jnp.sum(jnp.where(hit, slots, 0.0), axis=1, keepdims=True))
    panel = lax.broadcasted_iota(jnp.int32, (PANELS, PANELS), 0)
    stored = lax.broadcasted_iota(jnp.int32, (PANELS, PANELS), 1).astype(jnp.float32)
    columns.append(jnp.sum(jnp.where(map_ref[...] == panel, stored, 0.0), axis=1, keepdims=True))
    columns.append(jnp.zeros((PANELS, 7), jnp.float32))
    table_ref[...] = jnp.concatenate(columns, axis=1).astype(jnp.int32)


def plan(place, block_index, panel_map):
    return pl.pallas_call(
        plan_kernel,
        out_shape=(
            jax.ShapeDtypeStruct((8, HERE), jnp.int32),
            jax.ShapeDtypeStruct((PANELS, 16), jnp.int32),
        ),
        in_specs=[
            pl.BlockSpec(memory_space=pltpu.SMEM),
            pl.BlockSpec(memory_space=pltpu.VMEM),
            pl.BlockSpec(memory_space=pltpu.VMEM),
        ],
        out_specs=(pl.BlockSpec(memory_space=pltpu.VMEM), pl.BlockSpec(memory_space=pltpu.VMEM)),
        compiler_params=pltpu.CompilerParams(vmem_limit_bytes=16 << 20),
        name="plan",
    )(place, block_index, panel_map)


def exchange_kernel(lists_ref, act_ref, pool_ref, act, to_right, to_left, send, recv, load, own):
    me = lax.axis_index("cols")
    right, left = lax.rem(me + 1, GROUPS), lax.rem(me + GROUPS - 1, GROUPS)
    reads = []
    for s in range(HERE):
        reads.append(pltpu.make_async_copy(act_ref.at[:, pl.ds(s * TILE, TILE)], act.at[s], load.at[s]))
        reads[-1].start()
    barrier = pltpu.get_barrier_semaphore()
    for neighbour in (left, right):
        pl.semaphore_signal(barrier, inc=1, device_id={"cols": neighbour}, device_id_type=MESH)
    for read in reads:
        read.wait()

    def pack(row, buffer, start, stop):
        def one(s, carry):
            buffer[s] = act[lists_ref[row, s]]
            return carry

        lax.fori_loop(start, stop, one, 0)

    def ship(n, src, dst, to):
        copy = pltpu.make_async_remote_copy(
            src_ref=src,
            dst_ref=pool_ref.at[pl.ds(dst, src.shape[0])],
            send_sem=send.at[n],
            recv_sem=recv.at[n],
            device_id={"cols": to},
            device_id_type=MESH,
        )
        copy.start()
        return copy

    pack(0, to_right, 0, PASSED)
    pack(1, to_left, 0, PASSED)
    pl.semaphore_wait(barrier, 2)
    rest = LISTED - PASSED
    head_right = ship(0, to_right.at[pl.ds(0, PASSED)], LEFT, right)
    head_left = ship(1, to_left.at[pl.ds(0, PASSED)], RIGHT, left)
    pack(0, to_right, PASSED, LISTED)
    pack(1, to_left, PASSED, LISTED)
    tail_right = ship(2, to_right.at[pl.ds(PASSED, rest)], LEFT + PASSED, right)
    tail_left = ship(3, to_left.at[pl.ds(PASSED, rest)], RIGHT + PASSED, left)
    keep = pltpu.make_async_copy(act, pool_ref.at[pl.ds(OWN, HERE)], own)
    keep.start()
    head_right.wait_recv()
    on_right = ship(4, pool_ref.at[pl.ds(LEFT, PASSED)], FAR_LEFT, right)
    head_left.wait_recv()
    on_left = ship(5, pool_ref.at[pl.ds(RIGHT, PASSED)], FAR_RIGHT, left)
    head_right.wait_send()
    head_left.wait_send()
    keep.wait()
    for copy in (tail_right, tail_left, on_right, on_left):
        copy.wait()


def exchange(lists, activations):
    rows = activations.shape[0]
    return pl.pallas_call(
        exchange_kernel,
        out_shape=jax.ShapeDtypeStruct((SLOTS, rows, TILE), jnp.bfloat16),
        in_specs=[pl.BlockSpec(memory_space=pltpu.SMEM), pl.BlockSpec(memory_space=pl.ANY)],
        out_specs=pl.BlockSpec(memory_space=pl.ANY),
        scratch_shapes=[
            pltpu.VMEM((HERE, rows, TILE), jnp.bfloat16),
            pltpu.VMEM((LISTED, rows, TILE), jnp.bfloat16),
            pltpu.VMEM((LISTED, rows, TILE), jnp.bfloat16),
            pltpu.SemaphoreType.DMA((6,)),
            pltpu.SemaphoreType.DMA((6,)),
            pltpu.SemaphoreType.DMA((HERE,)),
            pltpu.SemaphoreType.DMA,
        ],
        compiler_params=pltpu.CompilerParams(
            collective_id=0, has_side_effects=True, vmem_limit_bytes=40 << 20
        ),
        cost_estimate=pl.CostEstimate(flops=0, bytes_accessed=600 << 20, transcendentals=0),
        name="exchange",
    )(lists, activations)


def sums_kernel(table_ref, *refs):
    taken, (weight_ref, bias_ref, live_ref, out_ref) = refs[:DEPTH], refs[DEPTH:]
    j = pl.program_id(0)
    inputs = jnp.concatenate([ref[0] for ref in taken], axis=1)
    weights = weight_ref[0].reshape(DEPTH * TILE, TILE)
    total = jnp.dot(inputs, weights, preferred_element_type=jnp.float32)
    total = jnp.clip(total + bias_ref[pl.ds(j, 1), :], 0.0, 32.0)
    out_ref[...] = jnp.where(live_ref[...] > 0.0, total, 0.0).astype(jnp.bfloat16)


def sums(table, pool, panels, bias, live):
    rows = pool.shape[1]
    taken = [
        pl.BlockSpec((1, rows, TILE), functools.partial(lambda k, j, t: (t[j, k], 0, 0), k))
        for k in range(DEPTH)
    ]
    return pl.pallas_call(
        sums_kernel,
        out_shape=jax.ShapeDtypeStruct((rows, PANELS * TILE), jnp.bfloat16),
        grid_spec=pltpu.PrefetchScalarGridSpec(
            num_scalar_prefetch=1,
            grid=(PANELS,),
            in_specs=taken
            + [
                pl.BlockSpec((1, DEPTH, TILE, TILE), lambda j, t: (t[j, DEPTH], 0, 0, 0)),
                pl.BlockSpec((PANELS, TILE), lambda j, t: (0, 0)),
                pl.BlockSpec((rows, 1), lambda j, t: (0, 0)),
            ],
            out_specs=pl.BlockSpec((rows, TILE), lambda j, t: (0, j)),
        ),
        compiler_params=pltpu.CompilerParams(vmem_limit_bytes=32 << 20),
        cost_estimate=pl.CostEstimate(flops=4 << 30, bytes_accessed=52 << 20, transcendentals=0),
        name="sums",
    )(table, *([pool] * DEPTH), panels, bias, live)


def general(activations, weight_tiles, panel_map, block_index, active_list, bias):
    row_count, local_width = activations.shape
    blocks_here = row_count // ROW_BLOCK
    listed = active_list[0]
    picked = jnp.minimum(listed, blocks_here - 1)
    gathered = lax.all_gather(activations, "cols", axis=1, tiled=True)
    compact = jnp.take(gathered.reshape(blocks_here, ROW_BLOCK, -1), picked, axis=0)
    slot_rows = compact.shape[0] * ROW_BLOCK
    tile_view = compact.reshape(slot_rows, -1, TILE)
    panels_here = panel_map.shape[1]
    columns = lax.axis_index("cols") * panels_here + panel_map[0]
    sources = jnp.take(block_index, columns, axis=0)
    panel_block = lax.all_gather(weight_tiles[0], "rows", axis=0, tiled=True)
    count_here = panel_block.shape[0]
    total = jnp.zeros((slot_rows, count_here, TILE), jnp.float32)
    for depth in range(panel_block.shape[1]):
        chosen = jnp.take(tile_view, sources[:, depth], axis=1)
        total = total + jnp.einsum(
            "mpt,pts->mps", chosen, panel_block[:, depth], preferred_element_type=jnp.float32
        )
    ordered = jnp.take(total, jnp.argsort(panel_map[0]), axis=1).reshape(slot_rows, -1)
    clamped = jnp.minimum(jnp.maximum(ordered + bias[None, :], 0.0), 32.0).astype(jnp.bfloat16)
    placing = (listed[:, None] == jnp.arange(blocks_here, dtype=jnp.int32)[None, :]).astype(
        jnp.bfloat16
    )
    spread = jnp.einsum(
        "sb,srw->brw",
        placing,
        clamped.reshape(listed.shape[0], ROW_BLOCK, -1),
        preferred_element_type=jnp.float32,
    )
    return spread.astype(jnp.bfloat16).reshape(row_count, -1)


def body(activations, weight_tiles, panel_map, block_index, active_list, bias):
    place = lax.axis_index("cols").astype(jnp.int32).reshape(1)
    lists, table = plan(place, block_index, panel_map)
    fits = (lists[2, 0] <= PASSED) & (lists[3, 0] <= LISTED)

    def sparse(lists, table, activations, weight_tiles, panel_map, block_index, active_list, bias):
        rows = activations.shape[0]
        panels = lax.all_gather(weight_tiles[0], "rows", axis=0, tiled=True)
        pool = exchange(lists, activations)
        at = jnp.arange(rows, dtype=jnp.int32) // ROW_BLOCK
        live = jnp.any(at[:, None] == active_list, axis=1, keepdims=True).astype(jnp.float32)
        return sums(table, pool, panels, bias.reshape(PANELS, TILE), live)

    def dense(lists, table, *rest):
        return general(*rest)

    return lax.cond(
        fits, sparse, dense, lists, table, activations, weight_tiles, panel_map, block_index, active_list, bias
    )


def solution(mesh):
    in_specs = (
        P("rows", "cols"),
        P("cols", "rows", None, None, None),
        P("cols", None),
        P(),
        P("rows", None),
        P("cols"),
    )
    out_specs = P("rows", "cols")
    return jax.shard_map(body, mesh=mesh, in_specs=in_specs, out_specs=out_specs, check_vma=False)
```

```python
import jax
import jax.numpy as jnp
from jax import lax
from jax.experimental import pallas as pl
from jax.experimental.pallas import tpu as pltpu
from jax.sharding import PartitionSpec as P

TILE = 128
ROW_BLOCK = 16
GROUPS = 4
PANELS = 64
DEPTH = 8
HERE = 128
LISTED = 98
PASSED = 48
OWN, LEFT = 0, HERE
RIGHT = LEFT + LISTED
FAR_LEFT = RIGHT + LISTED
FAR_RIGHT = FAR_LEFT + PASSED
SLOTS = FAR_RIGHT + PASSED
CHUNKS = (128, 96, 32)
MESH = pl.DeviceIdType.MESH


def plan_kernel(place_ref, index_ref, map_ref, lists_ref, table_ref):
    place = place_ref[0]
    blocks = GROUPS * HERE
    lane = lax.broadcasted_iota(jnp.int32, (GROUPS * PANELS, blocks), 1)
    named = jnp.zeros((GROUPS * PANELS, blocks), jnp.float32)
    for k in range(DEPTH):
        named = jnp.where(index_ref[:, k : k + 1] == lane, 1.0, named)
    need = [jnp.max(named[c * PANELS : (c + 1) * PANELS], axis=0, keepdims=True) for c in range(GROUPS)]

    def asked(distance):
        return jnp.concatenate(
            [need[(s + distance) % GROUPS][:, s * HERE : (s + 1) * HERE] for s in range(GROUPS)], axis=0
        )

    right, far, left = asked(1), asked(2), asked(3)
    row = lax.broadcasted_iota(jnp.int32, (HERE, HERE), 0)
    col = lax.broadcasted_iota(jnp.int32, (HERE, HERE), 1)
    before = (row < col).astype(jnp.bfloat16)

    def rank(flags):
        return jnp.dot(flags.astype(jnp.bfloat16), before, preferred_element_type=jnp.float32)

    def count(flags):
        return jnp.sum(flags, axis=1, keepdims=True)

    both = far * right * left
    none = far * (1.0 - right) * (1.0 - left)
    only_right = far * right * (1.0 - left)
    only_left = far * left * (1.0 - right)
    none_n, both_n = count(none), count(both)
    cut = jnp.clip(jnp.floor((count(left) - count(right) + none_n) * 0.5), 0.0, none_n)
    tilt = count(only_left) + none_n - cut - count(only_right) - cut
    share = jnp.clip(jnp.floor((tilt + both_n) * 0.5), 0.0, both_n)
    by_right = only_right + none * (rank(none) < cut) + both * (rank(both) < share)
    by_left = far - by_right

    def order(passed, wanted):
        rest = wanted * (1.0 - passed)
        at = jnp.where(passed > 0.0, rank(passed), count(passed) + rank(rest))
        inside = passed + rest
        return jnp.where(inside > 0.0, at, -1.0), count(passed), count(inside)

    at_right, passed_right, listed_right = order(by_right, right)
    at_left, passed_left, listed_left = order(by_left, left)
    passed_most = jnp.max(jnp.maximum(passed_right, passed_left), axis=0, keepdims=True)
    listed_most = jnp.max(jnp.maximum(listed_right, listed_left), axis=0, keepdims=True)

    source = lax.broadcasted_iota(jnp.int32, (GROUPS, HERE), 0)
    mine = source == place
    slot = lax.broadcasted_iota(jnp.int32, (HERE, HERE), 0).astype(jnp.float32)
    ids = lax.broadcasted_iota(jnp.int32, (8, HERE), 1).astype(jnp.bfloat16)

    def listing(at):
        own = jnp.sum(jnp.where(mine, at, 0.0), axis=0, keepdims=True)
        hot = (own == slot).astype(jnp.bfloat16)
        out = lax.dot_general(ids, hot, (((1,), (1,)), ((), ())), preferred_element_type=jnp.float32)
        return out[:1]

    lists_ref[...] = jnp.concatenate(
        [
            listing(at_right),
            listing(at_left),
            jnp.broadcast_to(passed_most, (1, HERE)),
            jnp.broadcast_to(listed_most, (1, HERE)),
            jnp.zeros((4, HERE), jnp.float32),
        ],
        axis=0,
    ).astype(jnp.int32)

    ids_here = lax.broadcasted_iota(jnp.int32, (GROUPS, HERE), 1).astype(jnp.float32)
    from_left = LEFT + at_right
    from_right = RIGHT + at_left
    from_far = jnp.where(by_right > 0.0, FAR_LEFT + at_right, FAR_RIGHT + at_left)
    away = lax.rem(source - place + GROUPS, GROUPS)
    slots = jnp.where(
        away == 0,
        OWN + ids_here,
        jnp.where(away == 1, from_right, jnp.where(away == 2, from_far, from_left)),
    )
    slots = jnp.concatenate([slots[s : s + 1] for s in range(GROUPS)], axis=1)
    mine_index = index_ref[pl.ds(pl.multiple_of(place * PANELS, PANELS), PANELS), :]
    lane = lax.broadcasted_iota(jnp.int32, (PANELS, blocks), 1)
    columns = []
    for k in range(DEPTH):
        hit = mine_index[:, k : k + 1] == lane
        columns.append(jnp.sum(jnp.where(hit, slots, 0.0), axis=1, keepdims=True))
    panel = lax.broadcasted_iota(jnp.int32, (PANELS, PANELS), 0)
    stored = lax.broadcasted_iota(jnp.int32, (PANELS, PANELS), 1).astype(jnp.float32)
    columns.append(jnp.sum(jnp.where(map_ref[...] == panel, stored, 0.0), axis=1, keepdims=True))
    columns.append(jnp.zeros((PANELS, 7), jnp.float32))
    table_ref[...] = jnp.concatenate(columns, axis=1).astype(jnp.int32)


def plan(place, block_index, panel_map):
    return pl.pallas_call(
        plan_kernel,
        out_shape=(
            jax.ShapeDtypeStruct((8, HERE), jnp.int32),
            jax.ShapeDtypeStruct((PANELS, 16), jnp.int32),
        ),
        in_specs=[
            pl.BlockSpec(memory_space=pltpu.SMEM),
            pl.BlockSpec(memory_space=pltpu.VMEM),
            pl.BlockSpec(memory_space=pltpu.VMEM),
        ],
        out_specs=(pl.BlockSpec(memory_space=pltpu.VMEM), pl.BlockSpec(memory_space=pltpu.VMEM)),
        compiler_params=pltpu.CompilerParams(vmem_limit_bytes=16 << 20),
        name="plan",
    )(place, block_index, panel_map)


def neighbours():
    me = lax.axis_index("cols")
    return lax.rem(me + 1, GROUPS), lax.rem(me + GROUPS - 1, GROUPS)


def greet(right, left):
    barrier = pltpu.get_barrier_semaphore()
    for neighbour in (left, right):
        pl.semaphore_signal(barrier, inc=1, device_id={"cols": neighbour}, device_id_type=MESH)
    return barrier


class Trade:
    def __init__(self, lists_ref, act, pool, to_right, to_left, send, recv):
        self.lists_ref, self.act, self.pool = lists_ref, act, pool
        self.to_right, self.to_left, self.send, self.recv = to_right, to_left, send, recv
        self.right, self.left = neighbours()

    def pack(self, start, stop):
        def one(s, carry):
            self.to_right[s] = self.act[self.lists_ref[0, s]]
            self.to_left[s] = self.act[self.lists_ref[1, s]]
            return carry

        lax.fori_loop(start, stop, one, 0)

    def ship(self, n, src, dst, to):
        copy = pltpu.make_async_remote_copy(
            src_ref=src,
            dst_ref=self.pool.at[pl.ds(dst, src.shape[0])],
            send_sem=self.send.at[n],
            recv_sem=self.recv.at[n],
            device_id={"cols": to},
            device_id_type=MESH,
        )
        copy.start()
        return copy

    def heads(self):
        self.head_right = self.ship(0, self.to_right.at[pl.ds(0, PASSED)], LEFT, self.right)
        self.head_left = self.ship(1, self.to_left.at[pl.ds(0, PASSED)], RIGHT, self.left)

    def tails(self):
        rest = LISTED - PASSED
        self.tail_right = self.ship(2, self.to_right.at[pl.ds(PASSED, rest)], LEFT + PASSED, self.right)
        self.tail_left = self.ship(3, self.to_left.at[pl.ds(PASSED, rest)], RIGHT + PASSED, self.left)

    def pass_on(self):
        self.head_right.wait_recv()
        self.on_right = self.ship(4, self.pool.at[pl.ds(LEFT, PASSED)], FAR_LEFT, self.right)
        self.head_left.wait_recv()
        self.on_left = self.ship(5, self.pool.at[pl.ds(RIGHT, PASSED)], FAR_RIGHT, self.left)

    def finish(self):
        self.head_right.wait_send()
        self.head_left.wait_send()
        for copy in (self.tail_right, self.tail_left, self.on_right, self.on_left):
            copy.wait()


def read_rows(act_ref, first, act, load):
    reads = []
    for s in range(HERE):
        rows = pl.ds(first, act.shape[1])
        reads.append(pltpu.make_async_copy(act_ref.at[rows, pl.ds(s * TILE, TILE)], act.at[s], load.at[s]))
        reads[-1].start()
    return reads


def wait_all(copies):
    for copy in copies:
        copy.wait()


def exchange_kernel(lists_ref, act_ref, pool_ref, act, to_right, to_left, send, recv, load, own):
    trade = Trade(lists_ref, act, pool_ref, to_right, to_left, send, recv)
    reads = read_rows(act_ref, 0, act, load)
    barrier = greet(trade.right, trade.left)
    wait_all(reads)
    trade.pack(0, PASSED)
    pl.semaphore_wait(barrier, 2)
    trade.heads()
    trade.pack(PASSED, LISTED)
    trade.tails()
    keep = pltpu.make_async_copy(act, pool_ref.at[pl.ds(OWN, HERE)], own)
    keep.start()
    trade.pass_on()
    keep.wait()
    trade.finish()


def trade_scratch(rows):
    return [
        pltpu.VMEM((HERE, rows, TILE), jnp.bfloat16),
        pltpu.VMEM((LISTED, rows, TILE), jnp.bfloat16),
        pltpu.VMEM((LISTED, rows, TILE), jnp.bfloat16),
        pltpu.SemaphoreType.DMA((6,)),
        pltpu.SemaphoreType.DMA((6,)),
        pltpu.SemaphoreType.DMA((HERE,)),
        pltpu.SemaphoreType.DMA,
    ]


def exchange(lists, activations):
    return pl.pallas_call(
        exchange_kernel,
        out_shape=jax.ShapeDtypeStruct((SLOTS, CHUNKS[0], TILE), jnp.bfloat16),
        in_specs=[pl.BlockSpec(memory_space=pltpu.SMEM), pl.BlockSpec(memory_space=pl.ANY)],
        out_specs=pl.BlockSpec(memory_space=pl.ANY),
        scratch_shapes=trade_scratch(CHUNKS[0]),
        compiler_params=pltpu.CompilerParams(
            collective_id=0, has_side_effects=True, vmem_limit_bytes=62 << 20
        ),
        cost_estimate=pl.CostEstimate(flops=0, bytes_accessed=300 << 20, transcendentals=0),
        name="exchange",
    )(lists, activations)


def sums(table_ref, pool, weights, bias_ref, out_ref, first):
    rows = pool.shape[1]
    unroll = 4

    def some(step, carry):
        for u in range(unroll):
            j = step * unroll + u
            inputs = jnp.concatenate([pool[table_ref[j, k]] for k in range(DEPTH)], axis=1)
            panel = weights[table_ref[j, DEPTH]].reshape(DEPTH * TILE, TILE)
            total = jnp.dot(inputs, panel, preferred_element_type=jnp.float32)
            total = jnp.clip(total + bias_ref[pl.ds(j, 1), :], 0.0, 32.0)
            at = pl.ds(pl.multiple_of(j * TILE, TILE), TILE)
            out_ref[pl.ds(first, rows), at] = total.astype(jnp.bfloat16)
        return carry

    lax.fori_loop(0, PANELS // unroll, some, 0)


def layer_kernel(lists_ref, table_ref, act_ref, pool_ref, panels_ref, bias_ref, out_ref, *scratch):
    per = 8
    chunks = [scratch[n * per : (n + 1) * per] for n in range(len(CHUNKS) - 1)]
    pool, weights, staged = scratch[-3:]
    trades, reads, firsts = [], [], []
    first = CHUNKS[0]
    for n, (landed, act, to_right, to_left, send, recv, load, own) in enumerate(chunks):
        trades.append(Trade(lists_ref, act, landed, to_right, to_left, send, recv))
        reads.append(read_rows(act_ref, first, act, load))
        firsts.append(first)
        first += CHUNKS[n + 1]
    barrier = greet(trades[0].right, trades[0].left)
    stage = [
        pltpu.make_async_copy(panels_ref, weights, staged.at[0]),
        pltpu.make_async_copy(pool_ref, pool, staged.at[1]),
    ]
    for copy in stage:
        copy.start()
    keeps = []
    for n, trade in enumerate(trades):
        wait_all(reads[n])
        trade.pack(0, PASSED)
        if n == 0:
            pl.semaphore_wait(barrier, 2)
        trade.heads()
        trade.pack(PASSED, LISTED)
        if n == 0:
            trade.tails()
        keeps.append(pltpu.make_async_copy(trade.act, trade.pool.at[pl.ds(OWN, HERE)], chunks[n][-1]))
        keeps[-1].start()
    wait_all(stage)
    sums(table_ref, pool, weights, bias_ref, out_ref, 0)
    for n, trade in enumerate(trades):
        trade.pass_on()
        if n + 1 < len(trades):
            trades[n + 1].tails()
    for n, trade in enumerate(trades):
        keeps[n].wait()
        trade.finish()
        sums(table_ref, trade.pool, weights, bias_ref, out_ref, firsts[n])


def layer(lists, table, activations, pool, panels, bias):
    rows = activations.shape[0]
    scratch = []
    for m in CHUNKS[1:]:
        scratch += [pltpu.VMEM((SLOTS, m, TILE), jnp.bfloat16)] + trade_scratch(m)
    scratch += [
        pltpu.VMEM(pool.shape, jnp.bfloat16),
        pltpu.VMEM(panels.shape, jnp.bfloat16),
        pltpu.SemaphoreType.DMA((2,)),
    ]
    return pl.pallas_call(
        layer_kernel,
        out_shape=jax.ShapeDtypeStruct((rows, PANELS * TILE), jnp.bfloat16),
        in_specs=[pl.BlockSpec(memory_space=pltpu.SMEM)] * 2
        + [pl.BlockSpec(memory_space=pl.ANY)] * 3
        + [pl.BlockSpec(memory_space=pltpu.VMEM)],
        out_specs=pl.BlockSpec(memory_space=pltpu.VMEM),
        scratch_shapes=scratch,
        compiler_params=pltpu.CompilerParams(
            collective_id=1, has_side_effects=True, vmem_limit_bytes=62 << 20
        ),
        cost_estimate=pl.CostEstimate(flops=4 << 30, bytes_accessed=300 << 20, transcendentals=0),
        name="layer",
    )(lists, table, activations, pool, panels, bias)


def general(activations, weight_tiles, panel_map, block_index, active_list, bias):
    row_count, local_width = activations.shape
    blocks_here = row_count // ROW_BLOCK
    listed = active_list[0]
    picked = jnp.minimum(listed, blocks_here - 1)
    gathered = lax.all_gather(activations, "cols", axis=1, tiled=True)
    compact = jnp.take(gathered.reshape(blocks_here, ROW_BLOCK, -1), picked, axis=0)
    slot_rows = compact.shape[0] * ROW_BLOCK
    tile_view = compact.reshape(slot_rows, -1, TILE)
    panels_here = panel_map.shape[1]
    columns = lax.axis_index("cols") * panels_here + panel_map[0]
    sources = jnp.take(block_index, columns, axis=0)
    panel_block = lax.all_gather(weight_tiles[0], "rows", axis=0, tiled=True)
    count_here = panel_block.shape[0]
    total = jnp.zeros((slot_rows, count_here, TILE), jnp.float32)
    for depth in range(panel_block.shape[1]):
        chosen = jnp.take(tile_view, sources[:, depth], axis=1)
        total = total + jnp.einsum(
            "mpt,pts->mps", chosen, panel_block[:, depth], preferred_element_type=jnp.float32
        )
    ordered = jnp.take(total, jnp.argsort(panel_map[0]), axis=1).reshape(slot_rows, -1)
    clamped = jnp.minimum(jnp.maximum(ordered + bias[None, :], 0.0), 32.0).astype(jnp.bfloat16)
    placing = (listed[:, None] == jnp.arange(blocks_here, dtype=jnp.int32)[None, :]).astype(
        jnp.bfloat16
    )
    spread = jnp.einsum(
        "sb,srw->brw",
        placing,
        clamped.reshape(listed.shape[0], ROW_BLOCK, -1),
        preferred_element_type=jnp.float32,
    )
    return spread.astype(jnp.bfloat16).reshape(row_count, -1)


def body(activations, weight_tiles, panel_map, block_index, active_list, bias):
    place = lax.axis_index("cols").astype(jnp.int32).reshape(1)
    lists, table = plan(place, block_index, panel_map)
    fits = (lists[2, 0] <= PASSED) & (lists[3, 0] <= LISTED)

    def sparse(lists, table, activations, weight_tiles, panel_map, block_index, active_list, bias):
        rows = activations.shape[0]
        panels = lax.all_gather(weight_tiles[0], "rows", axis=0, tiled=True)
        pool = exchange(lists, activations)
        out = layer(lists, table, activations, pool, panels, bias.reshape(PANELS, TILE))
        at = jnp.arange(rows, dtype=jnp.int32) // ROW_BLOCK
        live = jnp.any(at[:, None] == active_list, axis=1, keepdims=True)
        return jnp.where(live, out, jnp.zeros_like(out))

    def dense(lists, table, *rest):
        return general(*rest)

    return lax.cond(
        fits, sparse, dense, lists, table, activations, weight_tiles, panel_map, block_index, active_list, bias
    )


def solution(mesh):
    in_specs = (
        P("rows", "cols"),
        P("cols", "rows", None, None, None),
        P("cols", None),
        P(),
        P("rows", None),
        P("cols"),
    )
    out_specs = P("rows", "cols")
    return jax.shard_map(body, mesh=mesh, in_specs=in_specs, out_specs=out_specs, check_vma=False)
```

```python
import functools

import jax
import jax.numpy as jnp
from jax import lax
from jax.experimental import pallas as pl
from jax.experimental.pallas import tpu as pltpu
from jax.sharding import PartitionSpec as P

TILE = 128
ROW_BLOCK = 16
GROUPS = 4
PANELS = 64
DEPTH = 8
HERE = 128
LIMITS = ((46, 94), (50, 100))
OWN, LEFT = 0, HERE
CHUNKS = (128, 96, 32)
MESH = pl.DeviceIdType.MESH


class Sizes:
    def __init__(self, passed, listed):
        self.passed, self.listed = passed, listed
        self.right = LEFT + listed
        self.far_left = self.right + listed
        self.far_right = self.far_left + passed
        self.slots = self.far_right + passed


SIZES = tuple(Sizes(*limits) for limits in LIMITS)


def plan_kernel(place_ref, index_ref, map_ref, lists_ref, choice_ref, *table_refs):
    place = place_ref[0]
    blocks = GROUPS * HERE
    lane = lax.broadcasted_iota(jnp.int32, (GROUPS * PANELS, blocks), 1)
    named = jnp.zeros((GROUPS * PANELS, blocks), jnp.float32)
    for k in range(DEPTH):
        named = jnp.where(index_ref[:, k : k + 1] == lane, 1.0, named)
    need = [jnp.max(named[c * PANELS : (c + 1) * PANELS], axis=0, keepdims=True) for c in range(GROUPS)]

    def asked(distance):
        return jnp.concatenate(
            [need[(s + distance) % GROUPS][:, s * HERE : (s + 1) * HERE] for s in range(GROUPS)], axis=0
        )

    right, far, left = asked(1), asked(2), asked(3)
    row = lax.broadcasted_iota(jnp.int32, (HERE, HERE), 0)
    col = lax.broadcasted_iota(jnp.int32, (HERE, HERE), 1)
    before = (row < col).astype(jnp.bfloat16)

    def rank(flags):
        return jnp.dot(flags.astype(jnp.bfloat16), before, preferred_element_type=jnp.float32)

    def count(flags):
        return jnp.sum(flags, axis=1, keepdims=True)

    both = far * right * left
    none = far * (1.0 - right) * (1.0 - left)
    only_right = far * right * (1.0 - left)
    only_left = far * left * (1.0 - right)
    none_n, both_n = count(none), count(both)
    cut = jnp.clip(jnp.floor((count(left) - count(right) + none_n) * 0.5), 0.0, none_n)
    tilt = count(only_left) + none_n - cut - count(only_right) - cut
    share = jnp.clip(jnp.floor((tilt + both_n) * 0.5), 0.0, both_n)
    by_right = only_right + none * (rank(none) < cut) + both * (rank(both) < share)
    by_left = far - by_right

    def order(passed, wanted):
        rest = wanted * (1.0 - passed)
        at = jnp.where(passed > 0.0, rank(passed), count(passed) + rank(rest))
        inside = passed + rest
        return jnp.where(inside > 0.0, at, -1.0), count(passed), count(inside)

    at_right, passed_right, listed_right = order(by_right, right)
    at_left, passed_left, listed_left = order(by_left, left)
    passed_most = jnp.max(jnp.maximum(passed_right, passed_left))
    listed_most = jnp.max(jnp.maximum(listed_right, listed_left))
    choice = jnp.int32(len(SIZES))
    for n, size in reversed(list(enumerate(SIZES))):
        fits = (passed_most <= size.passed) & (listed_most <= size.listed)
        choice = jnp.where(fits, jnp.int32(n), choice)
    choice_ref[0] = choice

    source = lax.broadcasted_iota(jnp.int32, (GROUPS, HERE), 0)
    mine = source == place
    slot = lax.broadcasted_iota(jnp.int32, (HERE, HERE), 0).astype(jnp.float32)
    ids = lax.broadcasted_iota(jnp.int32, (8, HERE), 1).astype(jnp.bfloat16)

    def listing(at):
        own = jnp.sum(jnp.where(mine, at, 0.0), axis=0, keepdims=True)
        hot = (own == slot).astype(jnp.bfloat16)
        out = lax.dot_general(ids, hot, (((1,), (1,)), ((), ())), preferred_element_type=jnp.float32)
        return out[:1]

    lists_ref[...] = jnp.concatenate(
        [
            listing(at_right),
            listing(at_left),
            jnp.zeros((6, HERE), jnp.float32),
        ],
        axis=0,
    ).astype(jnp.int32)

    ids_here = lax.broadcasted_iota(jnp.int32, (GROUPS, HERE), 1).astype(jnp.float32)
    away = lax.rem(source - place + GROUPS, GROUPS)
    mine_index = index_ref[pl.ds(pl.multiple_of(place * PANELS, PANELS), PANELS), :]
    lane = lax.broadcasted_iota(jnp.int32, (PANELS, blocks), 1)
    panel = lax.broadcasted_iota(jnp.int32, (PANELS, PANELS), 0)
    stored = lax.broadcasted_iota(jnp.int32, (PANELS, PANELS), 1).astype(jnp.float32)
    served = jnp.sum(jnp.where(map_ref[...] == panel, stored, 0.0), axis=1, keepdims=True)
    for size, table_ref in zip(SIZES, table_refs):
        from_far = jnp.where(by_right > 0.0, size.far_left + at_right, size.far_right + at_left)
        near = jnp.where(away == 1, size.right + at_left, LEFT + at_right)
        slots = jnp.where(away == 0, OWN + ids_here, jnp.where(away == 2, from_far, near))
        slots = jnp.concatenate([slots[s : s + 1] for s in range(GROUPS)], axis=1)
        columns = []
        for k in range(DEPTH):
            hit = mine_index[:, k : k + 1] == lane
            columns.append(jnp.sum(jnp.where(hit, slots, 0.0), axis=1, keepdims=True))
        columns += [served, jnp.zeros((PANELS, 7), jnp.float32)]
        table_ref[...] = jnp.concatenate(columns, axis=1).astype(jnp.int32)


def plan(place, block_index, panel_map):
    return pl.pallas_call(
        plan_kernel,
        out_shape=(
            jax.ShapeDtypeStruct((8, HERE), jnp.int32),
            jax.ShapeDtypeStruct((1,), jnp.int32),
        )
        + (jax.ShapeDtypeStruct((PANELS, 16), jnp.int32),) * len(SIZES),
        in_specs=[
            pl.BlockSpec(memory_space=pltpu.SMEM),
            pl.BlockSpec(memory_space=pltpu.VMEM),
            pl.BlockSpec(memory_space=pltpu.VMEM),
        ],
        out_specs=(
            pl.BlockSpec(memory_space=pltpu.VMEM),
            pl.BlockSpec(memory_space=pltpu.SMEM),
        )
        + (pl.BlockSpec(memory_space=pltpu.VMEM),) * len(SIZES),
        compiler_params=pltpu.CompilerParams(vmem_limit_bytes=16 << 20),
        name="plan",
    )(place, block_index, panel_map)


def neighbours():
    me = lax.axis_index("cols")
    return lax.rem(me + 1, GROUPS), lax.rem(me + GROUPS - 1, GROUPS)


def greet(right, left):
    barrier = pltpu.get_barrier_semaphore()
    for neighbour in (left, right):
        pl.semaphore_signal(barrier, inc=1, device_id={"cols": neighbour}, device_id_type=MESH)
    return barrier


class Trade:
    def __init__(self, size, lists_ref, act, pool, to_right, to_left, send, recv):
        self.lists_ref, self.act, self.pool = lists_ref, act, pool
        self.to_right, self.to_left, self.send, self.recv = to_right, to_left, send, recv
        self.size = size
        self.right, self.left = neighbours()

    def pack(self, start, stop):
        def one(s, carry):
            self.to_right[s] = self.act[self.lists_ref[0, s]]
            self.to_left[s] = self.act[self.lists_ref[1, s]]
            return carry

        lax.fori_loop(start, stop, one, 0)

    def ship(self, n, src, dst, to):
        copy = pltpu.make_async_remote_copy(
            src_ref=src,
            dst_ref=self.pool.at[pl.ds(dst, src.shape[0])],
            send_sem=self.send.at[n],
            recv_sem=self.recv.at[n],
            device_id={"cols": to},
            device_id_type=MESH,
        )
        copy.start()
        return copy

    def heads(self):
        first = pl.ds(0, self.size.passed)
        self.head_right = self.ship(0, self.to_right.at[first], LEFT, self.right)
        self.head_left = self.ship(1, self.to_left.at[first], self.size.right, self.left)

    def tails(self):
        passed = self.size.passed
        rest = pl.ds(passed, self.size.listed - passed)
        self.tail_right = self.ship(2, self.to_right.at[rest], LEFT + passed, self.right)
        self.tail_left = self.ship(3, self.to_left.at[rest], self.size.right + passed, self.left)

    def pass_on(self):
        size = self.size
        self.head_right.wait_recv()
        self.on_right = self.ship(4, self.pool.at[pl.ds(LEFT, size.passed)], size.far_left, self.right)
        self.head_left.wait_recv()
        self.on_left = self.ship(5, self.pool.at[pl.ds(size.right, size.passed)], size.far_right, self.left)

    def finish(self):
        self.head_right.wait_send()
        self.head_left.wait_send()
        for copy in (self.tail_right, self.tail_left, self.on_right, self.on_left):
            copy.wait()


def read_rows(act_ref, first, act, load):
    reads = []
    for s in range(HERE):
        rows = pl.ds(first, act.shape[1])
        reads.append(pltpu.make_async_copy(act_ref.at[rows, pl.ds(s * TILE, TILE)], act.at[s], load.at[s]))
        reads[-1].start()
    return reads


def wait_all(copies):
    for copy in copies:
        copy.wait()


def exchange_kernel(size, lists_ref, act_ref, pool_ref, act, to_right, to_left, send, recv, load, own):
    trade = Trade(size, lists_ref, act, pool_ref, to_right, to_left, send, recv)
    reads = read_rows(act_ref, 0, act, load)
    barrier = greet(trade.right, trade.left)
    wait_all(reads)
    trade.pack(0, size.passed)
    pl.semaphore_wait(barrier, 2)
    trade.heads()
    trade.pack(size.passed, size.listed)
    trade.tails()
    keep = pltpu.make_async_copy(act, pool_ref.at[pl.ds(OWN, HERE)], own)
    keep.start()
    trade.pass_on()
    keep.wait()
    trade.finish()


def trade_scratch(size, rows):
    return [
        pltpu.VMEM((HERE, rows, TILE), jnp.bfloat16),
        pltpu.VMEM((size.listed, rows, TILE), jnp.bfloat16),
        pltpu.VMEM((size.listed, rows, TILE), jnp.bfloat16),
        pltpu.SemaphoreType.DMA((6,)),
        pltpu.SemaphoreType.DMA((6,)),
        pltpu.SemaphoreType.DMA((HERE,)),
        pltpu.SemaphoreType.DMA,
    ]


def exchange(n, lists, activations):
    size = SIZES[n]
    return pl.pallas_call(
        functools.partial(exchange_kernel, size),
        out_shape=jax.ShapeDtypeStruct((size.slots, CHUNKS[0], TILE), jnp.bfloat16),
        in_specs=[pl.BlockSpec(memory_space=pltpu.SMEM), pl.BlockSpec(memory_space=pl.ANY)],
        out_specs=pl.BlockSpec(memory_space=pl.ANY),
        scratch_shapes=trade_scratch(size, CHUNKS[0]),
        compiler_params=pltpu.CompilerParams(
            collective_id=2 * n, has_side_effects=True, vmem_limit_bytes=62 << 20
        ),
        cost_estimate=pl.CostEstimate(flops=0, bytes_accessed=300 << 20, transcendentals=0),
        name="exchange",
    )(lists, activations)


def sums(table_ref, pool, weights, bias_ref, out_ref, first):
    rows = pool.shape[1]
    unroll = 4

    def some(step, carry):
        for u in range(unroll):
            j = step * unroll + u
            inputs = jnp.concatenate([pool[table_ref[j, k]] for k in range(DEPTH)], axis=1)
            panel = weights[table_ref[j, DEPTH]].reshape(DEPTH * TILE, TILE)
            total = jnp.dot(inputs, panel, preferred_element_type=jnp.float32)
            total = jnp.clip(total + bias_ref[pl.ds(j, 1), :], 0.0, 32.0)
            at = pl.ds(pl.multiple_of(j * TILE, TILE), TILE)
            out_ref[pl.ds(first, rows), at] = total.astype(jnp.bfloat16)
        return carry

    lax.fori_loop(0, PANELS // unroll, some, 0)


def layer_kernel(size, lists_ref, table_ref, act_ref, pool_ref, panels_ref, bias_ref, out_ref, *scratch):
    per = 8
    chunks = [scratch[n * per : (n + 1) * per] for n in range(len(CHUNKS) - 1)]
    pool, weights, staged = scratch[-3:]
    trades, reads, firsts = [], [], []
    first = CHUNKS[0]
    for n, (landed, act, to_right, to_left, send, recv, load, own) in enumerate(chunks):
        trades.append(Trade(size, lists_ref, act, landed, to_right, to_left, send, recv))
        reads.append(read_rows(act_ref, first, act, load))
        firsts.append(first)
        first += CHUNKS[n + 1]
    barrier = greet(trades[0].right, trades[0].left)
    stage = [
        pltpu.make_async_copy(panels_ref, weights, staged.at[0]),
        pltpu.make_async_copy(pool_ref, pool, staged.at[1]),
    ]
    for copy in stage:
        copy.start()
    keeps = []
    for n, trade in enumerate(trades):
        wait_all(reads[n])
        trade.pack(0, size.passed)
        if n == 0:
            pl.semaphore_wait(barrier, 2)
        trade.heads()
        trade.pack(size.passed, size.listed)
        if n == 0:
            trade.tails()
        keeps.append(pltpu.make_async_copy(trade.act, trade.pool.at[pl.ds(OWN, HERE)], chunks[n][-1]))
        keeps[-1].start()
    wait_all(stage)
    sums(table_ref, pool, weights, bias_ref, out_ref, 0)
    for n, trade in enumerate(trades):
        trade.pass_on()
        if n + 1 < len(trades):
            trades[n + 1].tails()
    for n, trade in enumerate(trades):
        keeps[n].wait()
        trade.finish()
        sums(table_ref, trade.pool, weights, bias_ref, out_ref, firsts[n])


def layer(n, lists, table, activations, pool, panels, bias):
    size, rows = SIZES[n], activations.shape[0]
    scratch = []
    for m in CHUNKS[1:]:
        scratch += [pltpu.VMEM((size.slots, m, TILE), jnp.bfloat16)] + trade_scratch(size, m)
    scratch += [
        pltpu.VMEM(pool.shape, jnp.bfloat16),
        pltpu.VMEM(panels.shape, jnp.bfloat16),
        pltpu.SemaphoreType.DMA((2,)),
    ]
    return pl.pallas_call(
        functools.partial(layer_kernel, size),
        out_shape=jax.ShapeDtypeStruct((rows, PANELS * TILE), jnp.bfloat16),
        in_specs=[pl.BlockSpec(memory_space=pltpu.SMEM)] * 2
        + [pl.BlockSpec(memory_space=pl.ANY)] * 3
        + [pl.BlockSpec(memory_space=pltpu.VMEM)],
        out_specs=pl.BlockSpec(memory_space=pltpu.VMEM),
        scratch_shapes=scratch,
        compiler_params=pltpu.CompilerParams(
            collective_id=2 * n + 1, has_side_effects=True, vmem_limit_bytes=62 << 20
        ),
        cost_estimate=pl.CostEstimate(flops=4 << 30, bytes_accessed=300 << 20, transcendentals=0),
        name="layer",
    )(lists, table, activations, pool, panels, bias)


def general(activations, weight_tiles, panel_map, block_index, active_list, bias):
    row_count, local_width = activations.shape
    blocks_here = row_count // ROW_BLOCK
    listed = active_list[0]
    picked = jnp.minimum(listed, blocks_here - 1)
    gathered = lax.all_gather(activations, "cols", axis=1, tiled=True)
    compact = jnp.take(gathered.reshape(blocks_here, ROW_BLOCK, -1), picked, axis=0)
    slot_rows = compact.shape[0] * ROW_BLOCK
    tile_view = compact.reshape(slot_rows, -1, TILE)
    panels_here = panel_map.shape[1]
    columns = lax.axis_index("cols") * panels_here + panel_map[0]
    sources = jnp.take(block_index, columns, axis=0)
    panel_block = lax.all_gather(weight_tiles[0], "rows", axis=0, tiled=True)
    count_here = panel_block.shape[0]
    total = jnp.zeros((slot_rows, count_here, TILE), jnp.float32)
    for depth in range(panel_block.shape[1]):
        chosen = jnp.take(tile_view, sources[:, depth], axis=1)
        total = total + jnp.einsum(
            "mpt,pts->mps", chosen, panel_block[:, depth], preferred_element_type=jnp.float32
        )
    ordered = jnp.take(total, jnp.argsort(panel_map[0]), axis=1).reshape(slot_rows, -1)
    clamped = jnp.minimum(jnp.maximum(ordered + bias[None, :], 0.0), 32.0).astype(jnp.bfloat16)
    placing = (listed[:, None] == jnp.arange(blocks_here, dtype=jnp.int32)[None, :]).astype(
        jnp.bfloat16
    )
    spread = jnp.einsum(
        "sb,srw->brw",
        placing,
        clamped.reshape(listed.shape[0], ROW_BLOCK, -1),
        preferred_element_type=jnp.float32,
    )
    return spread.astype(jnp.bfloat16).reshape(row_count, -1)


def body(activations, weight_tiles, panel_map, block_index, active_list, bias):
    rows = activations.shape[0]
    place = lax.axis_index("cols").astype(jnp.int32).reshape(1)
    lists, choice, *tables = plan(place, block_index, panel_map)

    def sparse(n):
        def branch(lists, tables, activations, weight_tiles, panel_map, block_index, active_list, bias):
            panels = lax.all_gather(weight_tiles[0], "rows", axis=0, tiled=True)
            pool = exchange(n, lists, activations)
            return layer(n, lists, tables[n], activations, pool, panels, bias.reshape(PANELS, TILE))

        return branch

    def dense(lists, tables, *rest):
        return general(*rest)

    branches = [sparse(n) for n in range(len(SIZES))] + [dense]
    out = lax.switch(
        choice[0], branches, lists, tables, activations, weight_tiles, panel_map, block_index, active_list, bias
    )
    at = jnp.arange(rows, dtype=jnp.int32) // ROW_BLOCK
    live = jnp.any(at[:, None] == active_list, axis=1, keepdims=True)
    return jnp.where(live, out, jnp.zeros_like(out))


def solution(mesh):
    in_specs = (
        P("rows", "cols"),
        P("cols", "rows", None, None, None),
        P("cols", None),
        P(),
        P("rows", None),
        P("cols"),
    )
    out_specs = P("rows", "cols")
    return jax.shard_map(body, mesh=mesh, in_specs=in_specs, out_specs=out_specs, check_vma=False)
```

```python
import functools

import jax
import jax.numpy as jnp
from jax import lax
from jax.experimental import pallas as pl
from jax.experimental.pallas import tpu as pltpu
from jax.sharding import PartitionSpec as P

TILE = 128
ROW_BLOCK = 16
GROUPS = 4
PANELS = 64
DEPTH = 8
HERE = 128
LIMITS = ((44, 91), (45, 93), (47, 96), (50, 101))
OWN, LEFT = 0, HERE
CHUNKS = (128, 96, 32)
MESH = pl.DeviceIdType.MESH


class Sizes:
    def __init__(self, passed, listed):
        self.passed, self.listed = passed, listed
        self.right = LEFT + listed
        self.far_left = self.right + listed
        self.far_right = self.far_left + passed
        self.slots = self.far_right + passed


SIZES = tuple(Sizes(*limits) for limits in LIMITS)


def plan_kernel(place_ref, index_ref, map_ref, lists_ref, choice_ref, *refs):
    table_refs, index = refs[:-1], refs[-1]
    place = place_ref[0]
    blocks = GROUPS * HERE
    index[...] = jnp.transpose(index_ref[...])
    lane = lax.broadcasted_iota(jnp.int32, (GROUPS * PANELS, blocks), 1)
    named = jnp.zeros((GROUPS * PANELS, blocks), jnp.float32)
    for k in range(DEPTH):
        named = jnp.where(index[:, k : k + 1] == lane, 1.0, named)
    need = [jnp.max(named[c * PANELS : (c + 1) * PANELS], axis=0, keepdims=True) for c in range(GROUPS)]

    def asked(distance):
        return jnp.concatenate(
            [need[(s + distance) % GROUPS][:, s * HERE : (s + 1) * HERE] for s in range(GROUPS)], axis=0
        )

    right, far, left = asked(1), asked(2), asked(3)
    row = lax.broadcasted_iota(jnp.int32, (HERE, HERE), 0)
    col = lax.broadcasted_iota(jnp.int32, (HERE, HERE), 1)
    before = (row < col).astype(jnp.bfloat16)

    def rank(flags):
        return jnp.dot(flags.astype(jnp.bfloat16), before, preferred_element_type=jnp.float32)

    def count(flags):
        return jnp.sum(flags, axis=1, keepdims=True)

    both = far * right * left
    none = far * (1.0 - right) * (1.0 - left)
    only_right = far * right * (1.0 - left)
    only_left = far * left * (1.0 - right)
    none_n, both_n = count(none), count(both)
    cut = jnp.clip(jnp.floor((count(left) - count(right) + none_n) * 0.5), 0.0, none_n)
    tilt = count(only_left) + none_n - cut - count(only_right) - cut
    share = jnp.clip(jnp.floor((tilt + both_n) * 0.5), 0.0, both_n)
    by_right = only_right + none * (rank(none) < cut) + both * (rank(both) < share)
    by_left = far - by_right

    def order(passed, wanted):
        rest = wanted * (1.0 - passed)
        at = jnp.where(passed > 0.0, rank(passed), count(passed) + rank(rest))
        inside = passed + rest
        return jnp.where(inside > 0.0, at, -1.0), count(passed), count(inside)

    at_right, passed_right, listed_right = order(by_right, right)
    at_left, passed_left, listed_left = order(by_left, left)
    passed_most = jnp.max(jnp.maximum(passed_right, passed_left))
    listed_most = jnp.max(jnp.maximum(listed_right, listed_left))
    choice = jnp.int32(len(SIZES))
    for n, size in reversed(list(enumerate(SIZES))):
        fits = (passed_most <= size.passed) & (listed_most <= size.listed)
        choice = jnp.where(fits, jnp.int32(n), choice)
    choice_ref[0] = choice

    source = lax.broadcasted_iota(jnp.int32, (GROUPS, HERE), 0)
    mine = source == place
    slot = lax.broadcasted_iota(jnp.int32, (HERE, HERE), 0).astype(jnp.float32)
    ids = lax.broadcasted_iota(jnp.int32, (8, HERE), 1).astype(jnp.bfloat16)

    def listing(at):
        own = jnp.sum(jnp.where(mine, at, 0.0), axis=0, keepdims=True)
        hot = (own == slot).astype(jnp.bfloat16)
        out = lax.dot_general(ids, hot, (((1,), (1,)), ((), ())), preferred_element_type=jnp.float32)
        return out[:1]

    lists_ref[...] = jnp.concatenate(
        [
            listing(at_right),
            listing(at_left),
            jnp.zeros((6, HERE), jnp.float32),
        ],
        axis=0,
    ).astype(jnp.int32)

    ids_here = lax.broadcasted_iota(jnp.int32, (GROUPS, HERE), 1).astype(jnp.float32)
    away = lax.rem(source - place + GROUPS, GROUPS)
    mine_index = index[pl.ds(pl.multiple_of(place * PANELS, PANELS), PANELS), :]
    lane = lax.broadcasted_iota(jnp.int32, (PANELS, blocks), 1)
    panel = lax.broadcasted_iota(jnp.int32, (PANELS, PANELS), 0)
    stored = lax.broadcasted_iota(jnp.int32, (PANELS, PANELS), 1).astype(jnp.float32)
    served = jnp.sum(jnp.where(map_ref[...] == panel, stored, 0.0), axis=1, keepdims=True)
    for size, table_ref in zip(SIZES, table_refs):
        from_far = jnp.where(by_right > 0.0, size.far_left + at_right, size.far_right + at_left)
        near = jnp.where(away == 1, size.right + at_left, LEFT + at_right)
        slots = jnp.where(away == 0, OWN + ids_here, jnp.where(away == 2, from_far, near))
        slots = jnp.concatenate([slots[s : s + 1] for s in range(GROUPS)], axis=1)
        columns = []
        for k in range(DEPTH):
            hit = mine_index[:, k : k + 1] == lane
            columns.append(jnp.sum(jnp.where(hit, slots, 0.0), axis=1, keepdims=True))
        columns += [served, jnp.zeros((PANELS, 7), jnp.float32)]
        table_ref[...] = jnp.concatenate(columns, axis=1).astype(jnp.int32)


def plan(place, block_index, panel_map):
    return pl.pallas_call(
        plan_kernel,
        out_shape=(
            jax.ShapeDtypeStruct((8, HERE), jnp.int32),
            jax.ShapeDtypeStruct((1,), jnp.int32),
        )
        + (jax.ShapeDtypeStruct((PANELS, 16), jnp.int32),) * len(SIZES),
        in_specs=[
            pl.BlockSpec(memory_space=pltpu.SMEM),
            pl.BlockSpec(memory_space=pltpu.VMEM),
            pl.BlockSpec(memory_space=pltpu.VMEM),
        ],
        out_specs=(
            pl.BlockSpec(memory_space=pltpu.VMEM),
            pl.BlockSpec(memory_space=pltpu.SMEM),
        )
        + (pl.BlockSpec(memory_space=pltpu.VMEM),) * len(SIZES),
        scratch_shapes=[pltpu.VMEM((GROUPS * PANELS, DEPTH), jnp.int32)],
        compiler_params=pltpu.CompilerParams(vmem_limit_bytes=16 << 20),
        name="plan",
    )(place, block_index.T, panel_map)


def neighbours():
    me = lax.axis_index("cols")
    return lax.rem(me + 1, GROUPS), lax.rem(me + GROUPS - 1, GROUPS)


def greet(right, left):
    barrier = pltpu.get_barrier_semaphore()
    for neighbour in (left, right):
        pl.semaphore_signal(barrier, inc=1, device_id={"cols": neighbour}, device_id_type=MESH)
    return barrier


def pack(lists_ref, act, to_right, to_left, start, stop):
    def one(s, carry):
        to_right[s] = act[lists_ref[0, s]]
        to_left[s] = act[lists_ref[1, s]]
        return carry

    lax.fori_loop(start, stop, one, 0)


class Trade:
    def __init__(self, size, pool, to_right, to_left, send, recv):
        self.size, self.pool = size, pool
        self.to_right, self.to_left, self.send, self.recv = to_right, to_left, send, recv
        self.right, self.left = neighbours()

    def ship(self, n, src, dst, to):
        copy = pltpu.make_async_remote_copy(
            src_ref=src,
            dst_ref=self.pool.at[pl.ds(dst, src.shape[0])],
            send_sem=self.send.at[n],
            recv_sem=self.recv.at[n],
            device_id={"cols": to},
            device_id_type=MESH,
        )
        copy.start()
        return copy

    def heads(self):
        first = pl.ds(0, self.size.passed)
        self.head_right = self.ship(0, self.to_right.at[first], LEFT, self.right)
        self.head_left = self.ship(1, self.to_left.at[first], self.size.right, self.left)

    def tails(self):
        passed = self.size.passed
        rest = pl.ds(passed, self.size.listed - passed)
        self.tail_right = self.ship(2, self.to_right.at[rest], LEFT + passed, self.right)
        self.tail_left = self.ship(3, self.to_left.at[rest], self.size.right + passed, self.left)

    def pass_on(self):
        size = self.size
        self.head_right.wait_recv()
        self.on_right = self.ship(4, self.pool.at[pl.ds(LEFT, size.passed)], size.far_left, self.right)
        self.head_left.wait_recv()
        self.on_left = self.ship(5, self.pool.at[pl.ds(size.right, size.passed)], size.far_right, self.left)

    def finish(self):
        self.head_right.wait_send()
        self.head_left.wait_send()
        for copy in (self.tail_right, self.tail_left, self.on_right, self.on_left):
            copy.wait()


def read_rows(act_ref, first, act, load):
    reads = []
    for s in range(HERE):
        rows = pl.ds(first, act.shape[1])
        reads.append(pltpu.make_async_copy(act_ref.at[rows, pl.ds(s * TILE, TILE)], act.at[s], load.at[s]))
        reads[-1].start()
    return reads


def wait_all(copies):
    for copy in copies:
        copy.wait()


def exchange_kernel(size, lists_ref, act_ref, pool_ref, *refs):
    later = len(CHUNKS) - 1
    outs, scratch = refs[: 3 * later], refs[3 * later :]
    packed = scratch[: 3 * (later + 1)]
    send, recv, load, own = scratch[3 * (later + 1) :]
    act, to_right, to_left = packed[:3]
    trade = Trade(size, pool_ref, to_right, to_left, send, recv)
    reads = read_rows(act_ref, 0, act, load.at[0])
    barrier = greet(trade.right, trade.left)
    wait_all(reads)
    pack(lists_ref, act, to_right, to_left, 0, size.passed)
    pl.semaphore_wait(barrier, 2)
    trade.heads()
    pack(lists_ref, act, to_right, to_left, size.passed, size.listed)
    trade.tails()
    keeps = [pltpu.make_async_copy(act, pool_ref.at[pl.ds(OWN, HERE)], own.at[0])]
    keeps[0].start()
    first = CHUNKS[0]
    for n in range(1, later + 1):
        mine, right, left = packed[3 * n : 3 * n + 3]
        wait_all(read_rows(act_ref, first, mine, load.at[n]))
        pack(lists_ref, mine, right, left, 0, size.listed)
        for k, ref in enumerate((mine, right, left)):
            keeps.append(pltpu.make_async_copy(ref, outs[3 * (n - 1) + k], own.at[3 * n + k]))
            keeps[-1].start()
        first += CHUNKS[n]
    trade.pass_on()
    wait_all(keeps)
    trade.finish()


def packed_shapes(size, rows):
    return [(HERE, rows, TILE), (size.listed, rows, TILE), (size.listed, rows, TILE)]


def exchange(n, lists, activations):
    size = SIZES[n]
    shapes = [packed_shapes(size, m) for m in CHUNKS]
    out_shapes = [(size.slots, CHUNKS[0], TILE)] + sum(shapes[1:], [])
    return pl.pallas_call(
        functools.partial(exchange_kernel, size),
        out_shape=[jax.ShapeDtypeStruct(shape, jnp.bfloat16) for shape in out_shapes],
        in_specs=[pl.BlockSpec(memory_space=pltpu.SMEM), pl.BlockSpec(memory_space=pl.ANY)],
        out_specs=[pl.BlockSpec(memory_space=pl.ANY)] * len(out_shapes),
        scratch_shapes=[pltpu.VMEM(shape, jnp.bfloat16) for shape in sum(shapes, [])]
        + [
            pltpu.SemaphoreType.DMA((6,)),
            pltpu.SemaphoreType.DMA((6,)),
            pltpu.SemaphoreType.DMA((len(CHUNKS), HERE)),
            pltpu.SemaphoreType.DMA((3 * len(CHUNKS),)),
        ],
        compiler_params=pltpu.CompilerParams(
            collective_id=2 * n, has_side_effects=True, vmem_limit_bytes=62 << 20
        ),
        cost_estimate=pl.CostEstimate(flops=0, bytes_accessed=300 << 20, transcendentals=0),
        name="exchange",
    )(lists, activations)


def sums(table_ref, active_ref, pool, weights, bias_ref, out_ref, first):
    rows = pool.shape[1]
    unroll = 4
    at = lax.broadcasted_iota(jnp.int32, (rows, TILE), 0) // ROW_BLOCK + first // ROW_BLOCK
    live = at == active_ref[0, 0]
    for s in range(1, active_ref.shape[1]):
        live = live | (at == active_ref[0, s])
    most = jnp.where(live, 32.0, 0.0)

    def some(step, carry):
        for u in range(unroll):
            j = step * unroll + u
            inputs = jnp.concatenate([pool[table_ref[j, k]] for k in range(DEPTH)], axis=1)
            panel = weights[table_ref[j, DEPTH]].reshape(DEPTH * TILE, TILE)
            total = jnp.dot(inputs, panel, preferred_element_type=jnp.float32)
            total = jnp.minimum(jnp.maximum(total + bias_ref[pl.ds(j, 1), :], 0.0), most)
            at = pl.ds(pl.multiple_of(j * TILE, TILE), TILE)
            out_ref[pl.ds(first, rows), at] = total.astype(jnp.bfloat16)
        return carry

    lax.fori_loop(0, PANELS // unroll, some, 0)


def layer_kernel(size, table_ref, active_ref, pool_ref, panels_ref, bias_ref, *refs):
    later = len(CHUNKS) - 1
    ins, out_ref, scratch = refs[: 3 * later], refs[3 * later], refs[3 * later + 1 :]
    pools, (pool, weights, send, recv, staged) = scratch[:later], scratch[later:]
    trades, firsts = [], []
    first = CHUNKS[0]
    for n in range(later):
        mine, right, left = ins[3 * n : 3 * n + 3]
        trades.append(Trade(size, pools[n], right, left, send.at[n], recv.at[n]))
        firsts.append(first)
        first += CHUNKS[n + 1]
    barrier = greet(trades[0].right, trades[0].left)
    stage = [
        pltpu.make_async_copy(panels_ref, weights, staged.at[0]),
        pltpu.make_async_copy(pool_ref, pool, staged.at[1]),
    ]
    keeps = [
        pltpu.make_async_copy(ins[3 * n], pools[n].at[pl.ds(OWN, HERE)], staged.at[2 + n]) for n in range(later)
    ]
    pl.semaphore_wait(barrier, 2)
    trades[0].heads()
    trades[0].tails()
    for copy in stage + keeps:
        copy.start()
    for trade in trades[1:]:
        trade.heads()
    wait_all(stage)
    sums(table_ref, active_ref, pool, weights, bias_ref, out_ref, 0)
    for n, trade in enumerate(trades):
        trade.pass_on()
        if n + 1 < later:
            trades[n + 1].tails()
    for n, trade in enumerate(trades):
        keeps[n].wait()
        trade.finish()
        sums(table_ref, active_ref, trade.pool, weights, bias_ref, out_ref, firsts[n])


def layer(n, table, active_list, packed, panels, bias):
    size, later = SIZES[n], len(CHUNKS) - 1
    pool = packed[0]
    return pl.pallas_call(
        functools.partial(layer_kernel, size),
        out_shape=jax.ShapeDtypeStruct((sum(CHUNKS), PANELS * TILE), jnp.bfloat16),
        in_specs=[pl.BlockSpec(memory_space=pltpu.SMEM)] * 2
        + [pl.BlockSpec(memory_space=pl.ANY)] * 2
        + [pl.BlockSpec(memory_space=pltpu.VMEM)]
        + [pl.BlockSpec(memory_space=pl.ANY)] * (3 * later),
        out_specs=pl.BlockSpec(memory_space=pltpu.VMEM),
        scratch_shapes=[pltpu.VMEM((size.slots, m, TILE), jnp.bfloat16) for m in CHUNKS[1:]]
        + [
            pltpu.VMEM(pool.shape, jnp.bfloat16),
            pltpu.VMEM(panels.shape, jnp.bfloat16),
            pltpu.SemaphoreType.DMA((later, 6)),
            pltpu.SemaphoreType.DMA((later, 6)),
            pltpu.SemaphoreType.DMA((2 + later,)),
        ],
        compiler_params=pltpu.CompilerParams(
            collective_id=2 * n + 1, has_side_effects=True, vmem_limit_bytes=62 << 20
        ),
        cost_estimate=pl.CostEstimate(flops=4 << 30, bytes_accessed=300 << 20, transcendentals=0),
        name="layer",
    )(table, active_list, pool, panels, bias, *packed[1:])


def general(activations, weight_tiles, panel_map, block_index, active_list, bias):
    row_count, local_width = activations.shape
    blocks_here = row_count // ROW_BLOCK
    listed = active_list[0]
    picked = jnp.minimum(listed, blocks_here - 1)
    gathered = lax.all_gather(activations, "cols", axis=1, tiled=True)
    compact = jnp.take(gathered.reshape(blocks_here, ROW_BLOCK, -1), picked, axis=0)
    slot_rows = compact.shape[0] * ROW_BLOCK
    tile_view = compact.reshape(slot_rows, -1, TILE)
    panels_here = panel_map.shape[1]
    columns = lax.axis_index("cols") * panels_here + panel_map[0]
    sources = jnp.take(block_index, columns, axis=0)
    panel_block = lax.all_gather(weight_tiles[0], "rows", axis=0, tiled=True)
    count_here = panel_block.shape[0]
    total = jnp.zeros((slot_rows, count_here, TILE), jnp.float32)
    for depth in range(panel_block.shape[1]):
        chosen = jnp.take(tile_view, sources[:, depth], axis=1)
        total = total + jnp.einsum(
            "mpt,pts->mps", chosen, panel_block[:, depth], preferred_element_type=jnp.float32
        )
    ordered = jnp.take(total, jnp.argsort(panel_map[0]), axis=1).reshape(slot_rows, -1)
    clamped = jnp.minimum(jnp.maximum(ordered + bias[None, :], 0.0), 32.0).astype(jnp.bfloat16)
    placing = (listed[:, None] == jnp.arange(blocks_here, dtype=jnp.int32)[None, :]).astype(
        jnp.bfloat16
    )
    spread = jnp.einsum(
        "sb,srw->brw",
        placing,
        clamped.reshape(listed.shape[0], ROW_BLOCK, -1),
        preferred_element_type=jnp.float32,
    )
    return spread.astype(jnp.bfloat16).reshape(row_count, -1)


def body(activations, weight_tiles, panel_map, block_index, active_list, bias):
    place = lax.axis_index("cols").astype(jnp.int32).reshape(1)
    lists, choice, *tables = plan(place, block_index, panel_map)

    def sparse(n):
        def branch(lists, tables, activations, weight_tiles, panel_map, block_index, active_list, bias):
            panels = lax.all_gather(weight_tiles[0], "rows", axis=0, tiled=True)
            packed = exchange(n, lists, activations)
            return layer(n, tables[n], active_list, packed, panels, bias.reshape(PANELS, TILE))

        return branch

    def dense(lists, tables, *rest):
        return general(*rest)

    branches = [sparse(n) for n in range(len(SIZES))] + [dense]
    return lax.switch(
        choice[0], branches, lists, tables, activations, weight_tiles, panel_map, block_index, active_list, bias
    )


def solution(mesh):
    in_specs = (
        P("rows", "cols"),
        P("cols", "rows", None, None, None),
        P("cols", None),
        P(),
        P("rows", None),
        P("cols"),
    )
    out_specs = P("rows", "cols")
    return jax.shard_map(body, mesh=mesh, in_specs=in_specs, out_specs=out_specs, check_vma=False)
```

```python
import functools

import jax
import jax.numpy as jnp
from jax import lax
from jax.experimental import pallas as pl
from jax.experimental.pallas import tpu as pltpu
from jax.sharding import PartitionSpec as P

TILE = 128
ROW_BLOCK = 16
GROUPS = 4
PANELS = 64
DEPTH = 8
HERE = 128
LIMITS = ((46, 94), (50, 100))
OWN, LEFT = 0, HERE
BLOCKS = 16
UNIT = 8
RING = 4
FIRST = 8
SHARED = 14
SPARE = BLOCKS - SHARED
LATER = ((8, 1), (12, 2), (9, 3), (14, 2))
MIXED = 1
MESH = pl.DeviceIdType.MESH


class Sizes:
    def __init__(self, passed, listed):
        self.passed, self.listed = passed, listed
        self.right = LEFT + listed
        self.far_left = self.right + listed
        self.far_right = self.far_left + passed
        self.slots = self.far_right + passed


SIZES = tuple(Sizes(*limits) for limits in LIMITS)


def plan_kernel(place_ref, active_ref, index_ref, map_ref, weights_ref, lists_ref, choice_ref, *refs):
    table_refs, (held_ref, index, held, moved) = refs[:-4], refs[-4:]
    tiles = weights_ref.shape[0]
    bring = pltpu.make_async_copy(weights_ref, held.at[pl.ds(0, tiles)], moved.at[0])
    bring.start()
    column = lax.broadcasted_iota(jnp.int32, (ROW_BLOCK, TILE), 1)
    listed = jnp.zeros((ROW_BLOCK, TILE), jnp.int32)
    for s in range(BLOCKS):
        listed = jnp.where(column == s, active_ref[0, s], listed)
    held[pl.ds(tiles, ROW_BLOCK)] = listed.astype(jnp.float32).astype(jnp.bfloat16)
    bring.wait()
    leave = pltpu.make_async_copy(held, held_ref, moved.at[1])
    leave.start()
    place = place_ref[0]
    blocks = GROUPS * HERE
    index[...] = jnp.transpose(index_ref[...])
    lane = lax.broadcasted_iota(jnp.int32, (GROUPS * PANELS, blocks), 1)
    named = jnp.zeros((GROUPS * PANELS, blocks), jnp.float32)
    for k in range(DEPTH):
        named = jnp.where(index[:, k : k + 1] == lane, 1.0, named)
    need = [jnp.max(named[c * PANELS : (c + 1) * PANELS], axis=0, keepdims=True) for c in range(GROUPS)]

    def asked(distance):
        return jnp.concatenate(
            [need[(s + distance) % GROUPS][:, s * HERE : (s + 1) * HERE] for s in range(GROUPS)], axis=0
        )

    right, far, left = asked(1), asked(2), asked(3)
    row = lax.broadcasted_iota(jnp.int32, (HERE, HERE), 0)
    col = lax.broadcasted_iota(jnp.int32, (HERE, HERE), 1)
    before = (row < col).astype(jnp.bfloat16)

    def rank(flags):
        return jnp.dot(flags.astype(jnp.bfloat16), before, preferred_element_type=jnp.float32)

    def count(flags):
        return jnp.sum(flags, axis=1, keepdims=True)

    both = far * right * left
    none = far * (1.0 - right) * (1.0 - left)
    only_right = far * right * (1.0 - left)
    only_left = far * left * (1.0 - right)
    none_n, both_n = count(none), count(both)
    cut = jnp.clip(jnp.floor((count(left) - count(right) + none_n) * 0.5), 0.0, none_n)
    tilt = count(only_left) + none_n - cut - count(only_right) - cut
    share = jnp.clip(jnp.floor((tilt + both_n) * 0.5), 0.0, both_n)
    by_right = only_right + none * (rank(none) < cut) + both * (rank(both) < share)
    by_left = far - by_right

    def order(passed, wanted):
        rest = wanted * (1.0 - passed)
        at = jnp.where(passed > 0.0, rank(passed), count(passed) + rank(rest))
        inside = passed + rest
        return jnp.where(inside > 0.0, at, -1.0), count(passed), count(inside)

    at_right, passed_right, listed_right = order(by_right, right)
    at_left, passed_left, listed_left = order(by_left, left)
    passed_most = jnp.max(jnp.maximum(passed_right, passed_left))
    listed_most = jnp.max(jnp.maximum(listed_right, listed_left))
    choice = jnp.int32(len(SIZES))
    for n, size in reversed(list(enumerate(SIZES))):
        fits = (passed_most <= size.passed) & (listed_most <= size.listed)
        choice = jnp.where(fits, jnp.int32(n), choice)
    choice_ref[0] = choice

    source = lax.broadcasted_iota(jnp.int32, (GROUPS, HERE), 0)
    mine = source == place
    slot = lax.broadcasted_iota(jnp.int32, (HERE, HERE), 0).astype(jnp.float32)
    ids = lax.broadcasted_iota(jnp.int32, (8, HERE), 1).astype(jnp.bfloat16)

    def listing(at):
        own = jnp.sum(jnp.where(mine, at, 0.0), axis=0, keepdims=True)
        hot = (own == slot).astype(jnp.bfloat16)
        out = lax.dot_general(ids, hot, (((1,), (1,)), ((), ())), preferred_element_type=jnp.float32)
        return out[:1]

    lists_ref[...] = jnp.concatenate(
        [
            listing(at_right),
            listing(at_left),
            jnp.zeros((6, HERE), jnp.float32),
        ],
        axis=0,
    ).astype(jnp.int32)

    ids_here = lax.broadcasted_iota(jnp.int32, (GROUPS, HERE), 1).astype(jnp.float32)
    away = lax.rem(source - place + GROUPS, GROUPS)
    mine_index = index[pl.ds(pl.multiple_of(place * PANELS, PANELS), PANELS), :]
    lane = lax.broadcasted_iota(jnp.int32, (PANELS, blocks), 1)
    panel = lax.broadcasted_iota(jnp.int32, (PANELS, PANELS), 0)
    stored = lax.broadcasted_iota(jnp.int32, (PANELS, PANELS), 1).astype(jnp.float32)
    served = jnp.sum(jnp.where(map_ref[...] == panel, stored, 0.0), axis=1, keepdims=True)
    for size, table_ref in zip(SIZES, table_refs):
        from_far = jnp.where(by_right > 0.0, size.far_left + at_right, size.far_right + at_left)
        near = jnp.where(away == 1, size.right + at_left, LEFT + at_right)
        slots = jnp.where(away == 0, OWN + ids_here, jnp.where(away == 2, from_far, near))
        slots = jnp.concatenate([slots[s : s + 1] for s in range(GROUPS)], axis=1)
        columns = []
        for k in range(DEPTH):
            hit = mine_index[:, k : k + 1] == lane
            columns.append(jnp.sum(jnp.where(hit, slots, 0.0), axis=1, keepdims=True))
        holder = jnp.floor(served * 0.5)
        columns += [served - 2.0 * holder, holder, jnp.zeros((PANELS, 6), jnp.float32)]
        table_ref[...] = jnp.concatenate(columns, axis=1).astype(jnp.int32)
    leave.wait()


def plan(place, active_list, block_index, panel_map, tiles):
    held = (tiles.shape[0] + ROW_BLOCK, TILE)
    vmem, smem, anywhere = (pl.BlockSpec(memory_space=space) for space in (pltpu.VMEM, pltpu.SMEM, pl.ANY))
    return pl.pallas_call(
        plan_kernel,
        out_shape=(
            jax.ShapeDtypeStruct((8, HERE), jnp.int32),
            jax.ShapeDtypeStruct((1,), jnp.int32),
        )
        + (jax.ShapeDtypeStruct((PANELS, 16), jnp.int32),) * len(SIZES)
        + (jax.ShapeDtypeStruct(held, jnp.bfloat16),),
        in_specs=[smem, smem, vmem, vmem, anywhere],
        out_specs=(vmem, smem) + (vmem,) * len(SIZES) + (anywhere,),
        scratch_shapes=[
            pltpu.VMEM((GROUPS * PANELS, DEPTH), jnp.int32),
            pltpu.VMEM(held, jnp.bfloat16),
            pltpu.SemaphoreType.DMA((2,)),
        ],
        compiler_params=pltpu.CompilerParams(vmem_limit_bytes=16 << 20),
        name="plan",
    )(place, active_list, block_index.T, panel_map, tiles)


def neighbours():
    me = lax.axis_index("cols")
    return lax.rem(me + 1, GROUPS), lax.rem(me + GROUPS - 1, GROUPS)


class Place:
    def __init__(self):
        row = lax.axis_index("rows")
        self.unit = (row // UNIT) * UNIT
        self.at = row - self.unit
        self.ring, self.core = self.at // 2, lax.rem(self.at, 2)
        self.partner = self.unit + self.ring * 2 + 1 - self.core

    def along(self, distance):
        return lax.rem(self.ring + distance + RING, RING) * 2 + self.core

    def peers(self):
        return [self.unit + self.along(1), self.unit + self.along(-1), self.partner]


def greet(unit=None):
    barrier = pltpu.get_barrier_semaphore()
    others = [{"cols": neighbour} for neighbour in neighbours()]
    if unit is not None:
        others += [{"rows": peer} for peer in unit.peers()]
    for other in others:
        pl.semaphore_signal(barrier, inc=1, device_id=other, device_id_type=MESH)
    return barrier, len(others)


def remote(src, dst, send, recv, to):
    copy = pltpu.make_async_remote_copy(
        src_ref=src, dst_ref=dst, send_sem=send, recv_sem=recv, device_id=to, device_id_type=MESH
    )
    copy.start()
    return copy


def wait_all(copies):
    for copy in copies:
        copy.wait()


class Trade:
    def __init__(self, size, pool, to_right, to_left, send, recv):
        self.size, self.pool = size, pool
        self.to_right, self.to_left, self.send, self.recv = to_right, to_left, send, recv
        self.right, self.left = neighbours()

    def ship(self, n, src, dst, to):
        return remote(
            src, self.pool.at[pl.ds(dst, src.shape[0])], self.send.at[n], self.recv.at[n], {"cols": to}
        )

    def heads(self):
        first = pl.ds(0, self.size.passed)
        self.head_right = self.ship(0, self.to_right.at[first], LEFT, self.right)
        self.head_left = self.ship(1, self.to_left.at[first], self.size.right, self.left)

    def tails(self):
        passed = self.size.passed
        rest = pl.ds(passed, self.size.listed - passed)
        self.tail_right = self.ship(2, self.to_right.at[rest], LEFT + passed, self.right)
        self.tail_left = self.ship(3, self.to_left.at[rest], self.size.right + passed, self.left)

    def pass_on(self):
        size = self.size
        self.head_right.wait_recv()
        self.on_right = self.ship(4, self.pool.at[pl.ds(LEFT, size.passed)], size.far_left, self.right)
        self.head_left.wait_recv()
        self.on_left = self.ship(5, self.pool.at[pl.ds(size.right, size.passed)], size.far_right, self.left)

    def finish(self):
        self.head_right.wait_send()
        self.head_left.wait_send()
        wait_all((self.tail_right, self.tail_left, self.on_right, self.on_left))


class Spread:
    def __init__(self, unit, src, everyones, send, recv):
        self.unit, self.src, self.everyones, self.send, self.recv = unit, src, everyones, send, recv

    def start(self):
        self.copies = [self.ship(n, self.src, self.unit.at, peer) for n, peer in enumerate(self.unit.peers())]

    def ship(self, n, src, at, to):
        return remote(src, self.everyones.at[at], self.send.at[n], self.recv.at[n], {"rows": to})

    def again(self, n, distance, to):
        at = self.unit.along(distance)
        self.relayed.append(self.ship(n, self.everyones.at[at], at, to))

    def relay(self):
        self.relayed = []
        for copy in self.copies[:2]:
            copy.wait_recv()
        way = 1 - 2 * self.unit.core
        self.again(3, -way, self.unit.unit + self.unit.along(way))
        self.again(4, -1, self.unit.partner)
        self.again(5, 1, self.unit.partner)

    def relay_far(self):
        self.relayed[0].wait_recv()
        self.again(6, 2, self.unit.partner)

    def finish(self):
        for copy in self.copies[:2] + self.relayed[:1]:
            copy.wait_send()
        wait_all(self.copies[2:] + self.relayed[1:])


COPIES = 2 * RING - 1


def pack(lists_ref, slots, to_right, to_left, start, stop):
    def one(s, carry):
        to_right[s] = slots(lists_ref[0, s])
        to_left[s] = slots(lists_ref[1, s])
        return carry

    lax.fori_loop(start, stop, one, 0)


def compact(act, rows, to):
    def one(s, carry):
        for i, row in enumerate(rows):
            to[s, i] = act[s, row]
        return carry

    lax.fori_loop(0, to.shape[0], one, 0)


def exchange_kernel(size, lists_ref, active_ref, act_ref, pool_ref, spares_ref, *refs):
    groups = len(LATER)
    outs, scratch = refs[: 3 * groups], refs[3 * groups :]
    act, early, late, to_right, to_left = scratch[:5]
    packed = scratch[5 : 5 + 2 * groups]
    send, recv, spare_send, spare_recv, load, kept = scratch[5 + 2 * groups :]
    unit = Place()
    trade = Trade(size, pool_ref, to_right, to_left, send, recv)
    spread = Spread(unit, late.at[:, pl.ds(SHARED - FIRST, SPARE)], spares_ref, spare_send, spare_recv)

    def read(s):
        part = act_ref.at[:, :, pl.ds(pl.multiple_of(s * TILE, TILE), TILE)]
        return pltpu.make_async_copy(part, act.at[s], load.at[s])

    def begin(s, carry):
        read(s).start()
        return carry

    def end(s, carry):
        read(s).wait()
        return carry

    lax.fori_loop(0, HERE, begin, 0)
    barrier, met = greet(unit)
    rows = [jnp.minimum(active_ref[0, s], BLOCKS - 1) for s in range(BLOCKS)]
    lax.fori_loop(0, HERE, end, 0)
    compact(act, rows[:FIRST], early)
    pack(lists_ref, lambda block: early[block], to_right, to_left, 0, size.passed)
    pl.semaphore_wait(barrier, met)
    trade.heads()
    pack(lists_ref, lambda block: early[block], to_right, to_left, size.passed, size.listed)
    trade.tails()
    compact(act, rows[FIRST:], late)
    spread.start()
    keeps = [
        pltpu.make_async_copy(early, pool_ref.at[pl.ds(OWN, HERE)], kept.at[0]),
        pltpu.make_async_copy(spread.src, spares_ref.at[unit.at], kept.at[1]),
    ]
    for n, (first, slots) in enumerate(LATER):
        right, left = packed[2 * n : 2 * n + 2]
        part = pl.ds(first - FIRST, slots)
        pack(lists_ref, lambda block: late[block, part], right, left, 0, size.listed)
        for k, ref in enumerate((late.at[:, part], right, left)):
            keeps.append(pltpu.make_async_copy(ref, outs[3 * n + k], kept.at[2 + 3 * n + k]))
    for copy in keeps:
        copy.start()
    trade.pass_on()
    spread.relay()
    wait_all(keeps)
    spread.relay_far()
    trade.finish()
    spread.finish()


def packed_shapes(size, slots):
    return [(blocks, slots, ROW_BLOCK, TILE) for blocks in (HERE, size.listed, size.listed)]


def exchange(n, lists, active_list, activations):
    size = SIZES[n]
    width = activations.shape[1]
    later = [packed_shapes(size, slots) for _, slots in LATER]
    outs = [(size.slots, FIRST, ROW_BLOCK, TILE), (UNIT, HERE, SPARE, ROW_BLOCK, TILE)] + sum(later, [])
    scratch = [(HERE, slots, ROW_BLOCK, TILE) for slots in (BLOCKS, FIRST, BLOCKS - FIRST)]
    scratch += packed_shapes(size, FIRST)[1:] + sum([shapes[1:] for shapes in later], [])
    return pl.pallas_call(
        functools.partial(exchange_kernel, size),
        out_shape=[jax.ShapeDtypeStruct(shape, jnp.bfloat16) for shape in outs],
        in_specs=[pl.BlockSpec(memory_space=pltpu.SMEM)] * 2 + [pl.BlockSpec(memory_space=pl.ANY)],
        out_specs=[pl.BlockSpec(memory_space=pl.ANY)] * len(outs),
        scratch_shapes=[pltpu.VMEM(shape, jnp.bfloat16) for shape in scratch]
        + [
            pltpu.SemaphoreType.DMA((6,)),
            pltpu.SemaphoreType.DMA((6,)),
            pltpu.SemaphoreType.DMA((COPIES,)),
            pltpu.SemaphoreType.DMA((COPIES,)),
            pltpu.SemaphoreType.DMA((HERE,)),
            pltpu.SemaphoreType.DMA((2 + 3 * len(LATER),)),
        ],
        compiler_params=pltpu.CompilerParams(
            collective_id=3 * n, has_side_effects=True, vmem_limit_bytes=62 << 20
        ),
        cost_estimate=pl.CostEstimate(flops=0, bytes_accessed=300 << 20, transcendentals=0),
        name="exchange",
    )(lists, active_list, activations.reshape(BLOCKS, ROW_BLOCK, width))


def sums(table_ref, pool, weights, bias_ref, out_ref, slot):
    rows = pool.shape[1] * ROW_BLOCK
    unroll = 4

    def some(step, carry):
        for u in range(unroll):
            j = step * unroll + u
            taken = [pool[table_ref[j, k]].reshape(rows, TILE) for k in range(DEPTH)]
            panel = weights[table_ref[j, DEPTH], table_ref[j, DEPTH + 1]]
            total = jnp.dot(jnp.concatenate(taken, axis=1), panel, preferred_element_type=jnp.float32)
            total = jnp.clip(total + bias_ref[pl.ds(j, 1), :], 0.0, 32.0)
            at = pl.ds(pl.multiple_of(j * TILE, TILE), TILE)
            out_ref[pl.ds(slot * ROW_BLOCK, rows), at] = total.astype(jnp.bfloat16)
        return carry

    lax.fori_loop(0, PANELS // unroll, some, 0)


def levels(everyone_ref, unit):
    extra, room, extra_at, room_at = [], [], [jnp.int32(0)], [jnp.int32(0)]
    for v in range(UNIT):
        active = jnp.int32(0)
        for s in range(BLOCKS):
            active = active + jnp.where(everyone_ref[unit + v, s] < BLOCKS, 1, 0)
        extra.append(jnp.maximum(active - SHARED, 0))
        room.append(jnp.clip(SHARED - active, 0, SPARE))
        extra_at.append(extra_at[-1] + extra[-1])
        room_at.append(room_at[-1] + room[-1])
    return extra, room, extra_at, room_at


def hosted(everyone_ref, unit):
    extra, room, extra_at, room_at = levels(everyone_ref, unit.unit)
    mine, begin = jnp.int32(0), jnp.int32(0)
    for v in range(UNIT):
        mine = mine + jnp.where(unit.at == v, room[v], 0)
        begin = begin + jnp.where(unit.at == v, room_at[v], 0)
    guests = []
    for f in range(SPARE):
        turn = begin + f
        owner, which = jnp.int32(0), jnp.int32(0)
        for v in range(UNIT):
            hit = (turn >= extra_at[v]) & (turn < extra_at[v + 1])
            owner = owner + jnp.where(hit, v, 0)
            which = which + jnp.where(hit, turn - extra_at[v], 0)
        guests.append(((f < mine) & (turn < extra_at[UNIT]), owner, which))
    return guests


def layer_kernel(size, shared, lists_ref, everyone_ref, table_ref, pool_ref, spares_ref, panels_ref, bias_ref, *refs):
    groups = LATER[:-1] if shared else LATER
    count = len(groups)
    refs = list(refs)

    def take(n):
        part, refs[:n] = refs[:n], []
        return part

    ins, (out_ref,) = take(3 * count), take(1)
    returned_ref = take(1)[0] if shared else None
    pools, (pool, weights, send, recv, staged) = take(count), take(5)
    unit = Place() if shared else None
    lists = [ins[3 * n : 3 * n + 3] for n in range(count)]
    if shared:
        cast, mine, right, left, back_send, back_recv, cast_sem = refs
        given = lists[MIXED][0]
        lists[MIXED] = (mine, right, left)
        back = Spread(
            unit,
            out_ref.at[pl.ds(LATER[MIXED][0] * ROW_BLOCK, SPARE * ROW_BLOCK)],
            returned_ref,
            back_send,
            back_recv,
        )
    trades = [Trade(size, pools[n], lists[n][1], lists[n][2], send.at[n], recv.at[n]) for n in range(count)]
    barrier, met = greet(unit)
    loads = [
        pltpu.make_async_copy(panels_ref.at[:, pl.ds(n * DEPTH * TILE, DEPTH * TILE)], weights.at[n], staged.at[n])
        for n in range(weights.shape[0])
    ] + [pltpu.make_async_copy(pool_ref, pool, staged.at[2])]
    keeps = [
        pltpu.make_async_copy(lists[n][0], pools[n].at[pl.ds(OWN, HERE)], staged.at[3 + n]) for n in range(count)
    ]
    if shared:
        casting = [
            pltpu.make_async_copy(spares_ref, cast.at[pl.ds(0, UNIT)], cast_sem.at[0]),
            pltpu.make_async_copy(given, cast.at[UNIT], cast_sem.at[1]),
        ]
        for copy in casting:
            copy.start()
    pl.semaphore_wait(barrier, met)
    trades[0].heads()
    trades[0].tails()
    for n, copy in enumerate(keeps):
        if not (shared and n == MIXED):
            copy.start()
    if shared:
        guests = hosted(everyone_ref, unit)
        wait_all(casting)
        whose, which = [], []
        for i in range(SPARE):
            taken, owner, nth = guests[SPARE - 1 - i]
            whose.append(jnp.where(taken, owner, UNIT))
            which.append(jnp.where(taken, nth, i))

        def guest(s, carry):
            for i in range(SPARE):
                mine[s, i] = cast[whose[i], s, which[i]]
            return carry

        lax.fori_loop(0, HERE, guest, 0)
        pack(lists_ref, lambda block: mine[block], right, left, 0, size.listed)
        keeps[MIXED].start()
    trades[1].heads()
    trades[1].tails()
    for copy in loads:
        copy.start()
    trades[0].pass_on()
    wait_all(loads)
    sums(table_ref, pool, weights, bias_ref, out_ref, 0)
    trades[1].pass_on()
    for trade in trades[2:]:
        trade.heads()
        trade.tails()
    for n in [1, 0] + list(range(2, count)):
        trade = trades[n]
        keeps[n].wait()
        if n == 2:
            for other in trades[2:]:
                other.pass_on()
            if shared:
                back.relay()
        trade.finish()
        if shared and n == 2:
            back.relay_far()
        sums(table_ref, trade.pool, weights, bias_ref, out_ref, groups[n][0])
        if shared and n == MIXED:
            back.start()
    if shared:
        back.finish()


def layer(n, shared, lists, everyone, table, pool, spares, packed, panels, bias):
    size = SIZES[n]
    groups = LATER[:-1] if shared else LATER
    slots = SHARED if shared else BLOCKS
    width = PANELS * TILE
    outs = [jax.ShapeDtypeStruct((slots * ROW_BLOCK, width), jnp.bfloat16)]
    out_specs = [pl.BlockSpec(memory_space=pltpu.VMEM)]
    count = len(groups)
    scratch = [pltpu.VMEM((size.slots, m, ROW_BLOCK, TILE), jnp.bfloat16) for _, m in groups] + [
        pltpu.VMEM(pool.shape, jnp.bfloat16),
        pltpu.VMEM((2, panels.shape[0], DEPTH * TILE, TILE), jnp.bfloat16),
        pltpu.SemaphoreType.DMA((count, 6)),
        pltpu.SemaphoreType.DMA((count, 6)),
        pltpu.SemaphoreType.DMA((3 + count,)),
    ]
    if shared:
        outs.append(jax.ShapeDtypeStruct((UNIT, SPARE * ROW_BLOCK, width), jnp.bfloat16))
        out_specs.append(pl.BlockSpec(memory_space=pl.ANY))
        scratch += [pltpu.VMEM((UNIT + 1,) + spares.shape[1:], jnp.bfloat16)]
        scratch += [pltpu.VMEM(shape, jnp.bfloat16) for shape in packed_shapes(size, SPARE)]
        scratch += [
            pltpu.SemaphoreType.DMA((COPIES,)),
            pltpu.SemaphoreType.DMA((COPIES,)),
            pltpu.SemaphoreType.DMA((2,)),
        ]
    return pl.pallas_call(
        functools.partial(layer_kernel, size, shared),
        out_shape=outs,
        in_specs=[pl.BlockSpec(memory_space=pltpu.SMEM)] * 3
        + [pl.BlockSpec(memory_space=pl.ANY)] * 3
        + [pl.BlockSpec(memory_space=pltpu.VMEM)]
        + [pl.BlockSpec(memory_space=pl.ANY)] * (3 * count),
        out_specs=out_specs,
        scratch_shapes=scratch,
        compiler_params=pltpu.CompilerParams(
            collective_id=3 * n + (2 if shared else 1), has_side_effects=True, vmem_limit_bytes=62 << 20
        ),
        cost_estimate=pl.CostEstimate(flops=4 << 30, bytes_accessed=300 << 20, transcendentals=0),
        name="layer",
    )(lists, everyone, table, pool, spares, panels, bias, *packed[: 3 * count])


def place_kernel(shared, row_ref, everyone_ref, *refs):
    out_ref, returned_ref = refs[0], refs[1] if shared else None
    result_ref, stage, read, write = refs[-4:]
    row = row_ref[0]
    unit = (row // UNIT) * UNIT
    held = SHARED if shared else BLOCKS
    if shared:
        extra, room, extra_at, room_at = levels(everyone_ref, unit)
        begin = jnp.int32(0)
        for v in range(UNIT):
            begin = begin + jnp.where(row - unit == v, extra_at[v], 0)
    slots = []
    for b in range(BLOCKS):
        slot = jnp.int32(-1)
        for s in range(BLOCKS):
            slot = jnp.where(everyone_ref[row, s] == b, s, slot)
        slots.append(slot)

        @pl.when((slot >= 0) & (slot < held))
        def _():
            at = pl.multiple_of(slot * ROW_BLOCK, ROW_BLOCK)
            pltpu.make_async_copy(out_ref.at[pl.ds(at, ROW_BLOCK)], stage.at[b], read.at[b]).start()

        if shared:
            turn = begin + slot - SHARED
            host, nth = jnp.int32(0), jnp.int32(0)
            for v in range(UNIT):
                hit = (turn >= room_at[v]) & (turn < room_at[v + 1])
                host = host + jnp.where(hit, v, 0)
                nth = nth + jnp.where(hit, turn - room_at[v], 0)

            @pl.when(slot >= held)
            def _():
                at = pl.multiple_of((SPARE - 1 - nth) * ROW_BLOCK, ROW_BLOCK)
                pltpu.make_async_copy(returned_ref.at[host, pl.ds(at, ROW_BLOCK)], stage.at[b], read.at[b]).start()

    writes = []
    for b in range(BLOCKS):

        @pl.when(slots[b] < 0)
        def _():
            stage[b] = jnp.zeros(stage.shape[1:], stage.dtype)

        @pl.when(slots[b] >= 0)
        def _():
            pltpu.make_async_copy(out_ref.at[pl.ds(0, ROW_BLOCK)], stage.at[b], read.at[b]).wait()

        to = result_ref.at[pl.ds(b * ROW_BLOCK, ROW_BLOCK)]
        writes.append(pltpu.make_async_copy(stage.at[b], to, write.at[b]))
        writes[-1].start()
    wait_all(writes)


def place(shared, everyone, outs):
    row = lax.axis_index("rows").astype(jnp.int32).reshape(1)
    width = outs[0].shape[1]
    return pl.pallas_call(
        functools.partial(place_kernel, shared),
        out_shape=jax.ShapeDtypeStruct((BLOCKS * ROW_BLOCK, width), jnp.bfloat16),
        in_specs=[pl.BlockSpec(memory_space=pltpu.SMEM)] * 2 + [pl.BlockSpec(memory_space=pl.ANY)] * len(outs),
        out_specs=pl.BlockSpec(memory_space=pl.ANY),
        scratch_shapes=[
            pltpu.VMEM((BLOCKS, ROW_BLOCK, width), jnp.bfloat16),
            pltpu.SemaphoreType.DMA((BLOCKS,)),
            pltpu.SemaphoreType.DMA((BLOCKS,)),
        ],
        compiler_params=pltpu.CompilerParams(vmem_limit_bytes=62 << 20),
        name="place",
    )(row, everyone, *outs)


def general(activations, weight_tiles, panel_map, block_index, active_list, bias):
    row_count, local_width = activations.shape
    blocks_here = row_count // ROW_BLOCK
    listed = active_list[0]
    picked = jnp.minimum(listed, blocks_here - 1)
    gathered = lax.all_gather(activations, "cols", axis=1, tiled=True)
    compact = jnp.take(gathered.reshape(blocks_here, ROW_BLOCK, -1), picked, axis=0)
    slot_rows = compact.shape[0] * ROW_BLOCK
    tile_view = compact.reshape(slot_rows, -1, TILE)
    panels_here = panel_map.shape[1]
    columns = lax.axis_index("cols") * panels_here + panel_map[0]
    sources = jnp.take(block_index, columns, axis=0)
    panel_block = lax.all_gather(weight_tiles[0], "rows", axis=0, tiled=True)
    count_here = panel_block.shape[0]
    total = jnp.zeros((slot_rows, count_here, TILE), jnp.float32)
    for depth in range(panel_block.shape[1]):
        chosen = jnp.take(tile_view, sources[:, depth], axis=1)
        total = total + jnp.einsum(
            "mpt,pts->mps", chosen, panel_block[:, depth], preferred_element_type=jnp.float32
        )
    ordered = jnp.take(total, jnp.argsort(panel_map[0]), axis=1).reshape(slot_rows, -1)
    clamped = jnp.minimum(jnp.maximum(ordered + bias[None, :], 0.0), 32.0).astype(jnp.bfloat16)
    placing = (listed[:, None] == jnp.arange(blocks_here, dtype=jnp.int32)[None, :]).astype(
        jnp.bfloat16
    )
    spread = jnp.einsum(
        "sb,srw->brw",
        placing,
        clamped.reshape(listed.shape[0], ROW_BLOCK, -1),
        preferred_element_type=jnp.float32,
    )
    return spread.astype(jnp.bfloat16).reshape(row_count, -1)


def body(activations, weight_tiles, panel_map, block_index, active_list, bias):
    at = lax.axis_index("cols").astype(jnp.int32).reshape(1)
    lists, choice, *tables, held = plan(at, active_list, block_index, panel_map, weight_tiles.reshape(-1, TILE))

    def sparse(n):
        def branch(lists, tables, held, activations, weight_tiles, panel_map, block_index, active_list, bias):
            panels = lax.all_gather(held, "rows", axis=0, tiled=False)
            pool, spares, *packed = exchange(n, lists, active_list, activations)
            everyone = panels[:, held.shape[0] - ROW_BLOCK, :BLOCKS].astype(jnp.int32)
            active = jnp.sum(everyone < BLOCKS, axis=1, dtype=jnp.int32).reshape(-1, UNIT)
            left_over = jnp.maximum(active - SHARED, 0) - jnp.clip(SHARED - active, 0, SPARE)
            level = jnp.all(jnp.sum(left_over, axis=1) <= 0)
            biases = bias.reshape(PANELS, TILE)

            def finish(shared):
                def last(lists, everyone, table, pool, spares, packed, panels, biases):
                    outs = layer(n, shared, lists, everyone, table, pool, spares, packed, panels, biases)
                    return place(shared, everyone, outs)

                return last

            return lax.cond(
                level, finish(True), finish(False), lists, everyone, tables[n], pool, spares, packed, panels, biases
            )

        return branch

    def dense(lists, tables, held, *rest):
        return general(*rest)

    branches = [sparse(n) for n in range(len(SIZES))] + [dense]
    rest = (activations, weight_tiles, panel_map, block_index, active_list, bias)
    return lax.switch(choice[0], branches, lists, tables, held, *rest)


def solution(mesh):
    in_specs = (
        P("rows", "cols"),
        P("cols", "rows", None, None, None),
        P("cols", None),
        P(),
        P("rows", None),
        P("cols"),
    )
    out_specs = P("rows", "cols")
    return jax.shard_map(body, mesh=mesh, in_specs=in_specs, out_specs=out_specs, check_vma=False)
```

```python
import functools

import jax
import jax.numpy as jnp
from jax import lax
from jax.experimental import pallas as pl
from jax.experimental.pallas import tpu as pltpu
from jax.sharding import PartitionSpec as P

TILE = 128
ROW_BLOCK = 16
GROUPS = 4
PANELS = 64
DEPTH = 8
HERE = 128
LIMITS = ((45, 92), (47, 95), (50, 100))
OWN, LEFT = 0, HERE
BLOCKS = 16
UNIT = 8
RING = 4
FIRST = 8
SHARED = 14
SPARE = BLOCKS - SHARED
LATER = ((8, 1), (12, 2), (9, 3), (14, 2))
MIXED = 1
MESH = pl.DeviceIdType.MESH


class Sizes:
    def __init__(self, passed, listed):
        self.passed, self.listed = passed, listed
        self.right = LEFT + listed
        self.far_left = self.right + listed
        self.far_right = self.far_left + passed
        self.slots = self.far_right + passed


SIZES = tuple(Sizes(*limits) for limits in LIMITS)


def plan_kernel(place_ref, active_ref, index_ref, map_ref, weights_ref, lists_ref, choice_ref, *refs):
    table_refs, (held_ref, index, held, moved) = refs[:-4], refs[-4:]
    tiles = weights_ref.shape[0]
    bring = pltpu.make_async_copy(weights_ref, held.at[pl.ds(0, tiles)], moved.at[0])
    bring.start()
    column = lax.broadcasted_iota(jnp.int32, (ROW_BLOCK, TILE), 1)
    listed = jnp.zeros((ROW_BLOCK, TILE), jnp.int32)
    for s in range(BLOCKS):
        listed = jnp.where(column == s, active_ref[0, s], listed)
    held[pl.ds(tiles, ROW_BLOCK)] = listed.astype(jnp.float32).astype(jnp.bfloat16)
    place = place_ref[0]
    blocks = GROUPS * HERE
    index[...] = jnp.transpose(index_ref[...])
    lane = lax.broadcasted_iota(jnp.int32, (GROUPS * PANELS, blocks), 1)
    named = jnp.zeros((GROUPS * PANELS, blocks), jnp.float32)
    for k in range(DEPTH):
        named = jnp.where(index[:, k : k + 1] == lane, 1.0, named)
    need = [jnp.max(named[c * PANELS : (c + 1) * PANELS], axis=0, keepdims=True) for c in range(GROUPS)]

    def asked(distance):
        return jnp.concatenate(
            [need[(s + distance) % GROUPS][:, s * HERE : (s + 1) * HERE] for s in range(GROUPS)], axis=0
        )

    right, far, left = asked(1), asked(2), asked(3)
    row = lax.broadcasted_iota(jnp.int32, (HERE, HERE), 0)
    col = lax.broadcasted_iota(jnp.int32, (HERE, HERE), 1)
    before = (row < col).astype(jnp.bfloat16)

    def rank(flags):
        return jnp.dot(flags.astype(jnp.bfloat16), before, preferred_element_type=jnp.float32)

    def count(flags):
        return jnp.sum(flags, axis=1, keepdims=True)

    both = far * right * left
    none = far * (1.0 - right) * (1.0 - left)
    only_right = far * right * (1.0 - left)
    only_left = far * left * (1.0 - right)
    none_n, both_n = count(none), count(both)
    cut = jnp.clip(jnp.floor((count(left) - count(right) + none_n) * 0.5), 0.0, none_n)
    tilt = count(only_left) + none_n - cut - count(only_right) - cut
    share = jnp.clip(jnp.floor((tilt + both_n) * 0.5), 0.0, both_n)
    by_right = only_right + none * (rank(none) < cut) + both * (rank(both) < share)
    by_left = far - by_right

    def order(passed, wanted):
        rest = wanted * (1.0 - passed)
        at = jnp.where(passed > 0.0, rank(passed), count(passed) + rank(rest))
        inside = passed + rest
        return jnp.where(inside > 0.0, at, -1.0), count(passed), count(inside)

    at_right, passed_right, listed_right = order(by_right, right)
    at_left, passed_left, listed_left = order(by_left, left)
    passed_most = jnp.max(jnp.maximum(passed_right, passed_left))
    listed_most = jnp.max(jnp.maximum(listed_right, listed_left))
    choice = jnp.int32(len(SIZES))
    for n, size in reversed(list(enumerate(SIZES))):
        fits = (passed_most <= size.passed) & (listed_most <= size.listed)
        choice = jnp.where(fits, jnp.int32(n), choice)
    choice_ref[0] = choice
    bring.wait()
    leave = pltpu.make_async_copy(held, held_ref, moved.at[1])
    leave.start()

    source = lax.broadcasted_iota(jnp.int32, (GROUPS, HERE), 0)
    mine = source == place
    slot = lax.broadcasted_iota(jnp.int32, (HERE, HERE), 0).astype(jnp.float32)
    ids = lax.broadcasted_iota(jnp.int32, (8, HERE), 1).astype(jnp.bfloat16)

    def listing(at):
        own = jnp.sum(jnp.where(mine, at, 0.0), axis=0, keepdims=True)
        hot = (own == slot).astype(jnp.bfloat16)
        out = lax.dot_general(ids, hot, (((1,), (1,)), ((), ())), preferred_element_type=jnp.float32)
        return out[:1]

    lists_ref[...] = jnp.concatenate(
        [
            listing(at_right),
            listing(at_left),
            jnp.zeros((6, HERE), jnp.float32),
        ],
        axis=0,
    ).astype(jnp.int32)

    ids_here = lax.broadcasted_iota(jnp.int32, (GROUPS, HERE), 1).astype(jnp.float32)
    away = lax.rem(source - place + GROUPS, GROUPS)
    mine_index = index[pl.ds(pl.multiple_of(place * PANELS, PANELS), PANELS), :]
    lane = lax.broadcasted_iota(jnp.int32, (PANELS, blocks), 1)
    panel = lax.broadcasted_iota(jnp.int32, (PANELS, PANELS), 0)
    stored = lax.broadcasted_iota(jnp.int32, (PANELS, PANELS), 1).astype(jnp.float32)
    served = jnp.sum(jnp.where(map_ref[...] == panel, stored, 0.0), axis=1, keepdims=True)
    for size, table_ref in zip(SIZES, table_refs):
        from_far = jnp.where(by_right > 0.0, size.far_left + at_right, size.far_right + at_left)
        near = jnp.where(away == 1, size.right + at_left, LEFT + at_right)
        slots = jnp.where(away == 0, OWN + ids_here, jnp.where(away == 2, from_far, near))
        slots = jnp.concatenate([slots[s : s + 1] for s in range(GROUPS)], axis=1)
        columns = []
        for k in range(DEPTH):
            hit = mine_index[:, k : k + 1] == lane
            columns.append(jnp.sum(jnp.where(hit, slots, 0.0), axis=1, keepdims=True))
        holder = jnp.floor(served * 0.5)
        columns += [served - 2.0 * holder, holder, jnp.zeros((PANELS, 6), jnp.float32)]
        table_ref[...] = jnp.concatenate(columns, axis=1).astype(jnp.int32)
    leave.wait()


def plan(place, active_list, block_index, panel_map, tiles):
    held = (tiles.shape[0] + ROW_BLOCK, TILE)
    vmem, smem, anywhere = (pl.BlockSpec(memory_space=space) for space in (pltpu.VMEM, pltpu.SMEM, pl.ANY))
    return pl.pallas_call(
        plan_kernel,
        out_shape=(
            jax.ShapeDtypeStruct((8, HERE), jnp.int32),
            jax.ShapeDtypeStruct((1,), jnp.int32),
        )
        + (jax.ShapeDtypeStruct((PANELS, 16), jnp.int32),) * len(SIZES)
        + (jax.ShapeDtypeStruct(held, jnp.bfloat16),),
        in_specs=[smem, smem, vmem, vmem, anywhere],
        out_specs=(vmem, smem) + (vmem,) * len(SIZES) + (anywhere,),
        scratch_shapes=[
            pltpu.VMEM((GROUPS * PANELS, DEPTH), jnp.int32),
            pltpu.VMEM(held, jnp.bfloat16),
            pltpu.SemaphoreType.DMA((2,)),
        ],
        compiler_params=pltpu.CompilerParams(vmem_limit_bytes=16 << 20),
        name="plan",
    )(place, active_list, block_index.T, panel_map, tiles)


def neighbours():
    me = lax.axis_index("cols")
    return lax.rem(me + 1, GROUPS), lax.rem(me + GROUPS - 1, GROUPS)


class Place:
    def __init__(self):
        row = lax.axis_index("rows")
        self.unit = (row // UNIT) * UNIT
        self.at = row - self.unit
        self.ring, self.core = self.at // 2, lax.rem(self.at, 2)
        self.partner = self.unit + self.ring * 2 + 1 - self.core

    def along(self, distance):
        return lax.rem(self.ring + distance + RING, RING) * 2 + self.core

    def peers(self):
        return [self.unit + self.along(1), self.unit + self.along(-1), self.partner]


def greet(unit=None):
    barrier = pltpu.get_barrier_semaphore()
    others = [{"cols": neighbour} for neighbour in neighbours()]
    if unit is not None:
        others += [{"rows": peer} for peer in unit.peers()]
    for other in others:
        pl.semaphore_signal(barrier, inc=1, device_id=other, device_id_type=MESH)
    return barrier, len(others)


def remote(src, dst, send, recv, to):
    copy = pltpu.make_async_remote_copy(
        src_ref=src, dst_ref=dst, send_sem=send, recv_sem=recv, device_id=to, device_id_type=MESH
    )
    copy.start()
    return copy


def wait_all(copies):
    for copy in copies:
        copy.wait()


class Trade:
    def __init__(self, size, pool, to_right, to_left, send, recv):
        self.size, self.pool = size, pool
        self.to_right, self.to_left, self.send, self.recv = to_right, to_left, send, recv
        self.right, self.left = neighbours()

    def ship(self, n, src, dst, to):
        return remote(
            src, self.pool.at[pl.ds(dst, src.shape[0])], self.send.at[n], self.recv.at[n], {"cols": to}
        )

    def heads(self):
        first = pl.ds(0, self.size.passed)
        self.head_right = self.ship(0, self.to_right.at[first], LEFT, self.right)
        self.head_left = self.ship(1, self.to_left.at[first], self.size.right, self.left)

    def tails(self):
        passed = self.size.passed
        rest = pl.ds(passed, self.size.listed - passed)
        self.tail_right = self.ship(2, self.to_right.at[rest], LEFT + passed, self.right)
        self.tail_left = self.ship(3, self.to_left.at[rest], self.size.right + passed, self.left)

    def pass_on(self):
        size = self.size
        self.head_right.wait_recv()
        self.on_right = self.ship(4, self.pool.at[pl.ds(LEFT, size.passed)], size.far_left, self.right)
        self.head_left.wait_recv()
        self.on_left = self.ship(5, self.pool.at[pl.ds(size.right, size.passed)], size.far_right, self.left)

    def finish(self):
        self.head_right.wait_send()
        self.head_left.wait_send()
        wait_all((self.tail_right, self.tail_left, self.on_right, self.on_left))


class Spread:
    def __init__(self, unit, src, everyones, send, recv):
        self.unit, self.src, self.everyones, self.send, self.recv = unit, src, everyones, send, recv

    def start(self):
        self.copies = [self.ship(n, self.src, self.unit.at, peer) for n, peer in enumerate(self.unit.peers())]

    def ship(self, n, src, at, to):
        return remote(src, self.everyones.at[at], self.send.at[n], self.recv.at[n], {"rows": to})

    def again(self, n, distance, to):
        at = self.unit.along(distance)
        self.relayed.append(self.ship(n, self.everyones.at[at], at, to))

    def relay(self):
        self.relayed = []
        for copy in self.copies[:2]:
            copy.wait_recv()
        way = 1 - 2 * self.unit.core
        self.again(3, -way, self.unit.unit + self.unit.along(way))
        self.again(4, -1, self.unit.partner)
        self.again(5, 1, self.unit.partner)

    def relay_far(self):
        self.relayed[0].wait_recv()
        self.again(6, 2, self.unit.partner)

    def finish(self):
        for copy in self.copies[:2] + self.relayed[:1]:
            copy.wait_send()
        wait_all(self.copies[2:] + self.relayed[1:])


COPIES = 2 * RING - 1


def pack(lists_ref, slots, to_right, to_left, start, stop):
    def one(s, carry):
        to_right[s] = slots(lists_ref[0, s])
        to_left[s] = slots(lists_ref[1, s])
        return carry

    lax.fori_loop(start, stop, one, 0)


def compact(act, rows, to):
    def one(s, carry):
        for i, row in enumerate(rows):
            to[s, i] = act[s, row]
        return carry

    lax.fori_loop(0, to.shape[0], one, 0)


def exchange_kernel(size, lists_ref, active_ref, act_ref, pool_ref, spares_ref, *refs):
    groups = len(LATER)
    outs, scratch = refs[: 3 * groups], refs[3 * groups :]
    act, early, late, to_right, to_left = scratch[:5]
    packed = scratch[5 : 5 + 2 * groups]
    send, recv, spare_send, spare_recv, load, kept = scratch[5 + 2 * groups :]
    unit = Place()
    trade = Trade(size, pool_ref, to_right, to_left, send, recv)
    spread = Spread(unit, late.at[:, pl.ds(SHARED - FIRST, SPARE)], spares_ref, spare_send, spare_recv)

    def read(s):
        part = act_ref.at[:, :, pl.ds(pl.multiple_of(s * TILE, TILE), TILE)]
        return pltpu.make_async_copy(part, act.at[s], load.at[s])

    def begin(s, carry):
        read(s).start()
        return carry

    def end(s, carry):
        read(s).wait()
        return carry

    lax.fori_loop(0, HERE, begin, 0)
    barrier, met = greet(unit)
    rows = [jnp.minimum(active_ref[0, s], BLOCKS - 1) for s in range(BLOCKS)]
    lax.fori_loop(0, HERE, end, 0)

    def head(s, carry):
        a, b = lists_ref[0, s], lists_ref[1, s]
        for i in range(FIRST):
            to_right[s, i] = act[a, rows[i]]
            to_left[s, i] = act[b, rows[i]]
        return carry

    lax.fori_loop(0, size.passed, head, 0)
    pl.semaphore_wait(barrier, met)
    trade.heads()
    compact(act, rows[:FIRST], early)
    pack(lists_ref, lambda block: early[block], to_right, to_left, size.passed, size.listed)
    trade.tails()
    compact(act, rows[FIRST:], late)
    spread.start()
    keeps = [
        pltpu.make_async_copy(early, pool_ref.at[pl.ds(OWN, HERE)], kept.at[0]),
        pltpu.make_async_copy(spread.src, spares_ref.at[unit.at], kept.at[1]),
    ]
    for n, (first, slots) in enumerate(LATER):
        right, left = packed[2 * n : 2 * n + 2]
        part = pl.ds(first - FIRST, slots)
        pack(lists_ref, lambda block: late[block, part], right, left, 0, size.listed)
        for k, ref in enumerate((late.at[:, part], right, left)):
            keeps.append(pltpu.make_async_copy(ref, outs[3 * n + k], kept.at[2 + 3 * n + k]))
    for copy in keeps:
        copy.start()
    trade.pass_on()
    spread.relay()
    wait_all(keeps)
    spread.relay_far()
    trade.finish()
    spread.finish()


def packed_shapes(size, slots):
    return [(blocks, slots, ROW_BLOCK, TILE) for blocks in (HERE, size.listed, size.listed)]


def exchange(n, lists, active_list, activations):
    size = SIZES[n]
    width = activations.shape[1]
    later = [packed_shapes(size, slots) for _, slots in LATER]
    outs = [(size.slots, FIRST, ROW_BLOCK, TILE), (UNIT, HERE, SPARE, ROW_BLOCK, TILE)] + sum(later, [])
    scratch = [(HERE, slots, ROW_BLOCK, TILE) for slots in (BLOCKS, FIRST, BLOCKS - FIRST)]
    scratch += packed_shapes(size, FIRST)[1:] + sum([shapes[1:] for shapes in later], [])
    return pl.pallas_call(
        functools.partial(exchange_kernel, size),
        out_shape=[jax.ShapeDtypeStruct(shape, jnp.bfloat16) for shape in outs],
        in_specs=[pl.BlockSpec(memory_space=pltpu.SMEM)] * 2 + [pl.BlockSpec(memory_space=pl.ANY)],
        out_specs=[pl.BlockSpec(memory_space=pl.ANY)] * len(outs),
        scratch_shapes=[pltpu.VMEM(shape, jnp.bfloat16) for shape in scratch]
        + [
            pltpu.SemaphoreType.DMA((6,)),
            pltpu.SemaphoreType.DMA((6,)),
            pltpu.SemaphoreType.DMA((COPIES,)),
            pltpu.SemaphoreType.DMA((COPIES,)),
            pltpu.SemaphoreType.DMA((HERE,)),
            pltpu.SemaphoreType.DMA((2 + 3 * len(LATER),)),
        ],
        compiler_params=pltpu.CompilerParams(
            collective_id=3 * n, has_side_effects=True, vmem_limit_bytes=62 << 20
        ),
        cost_estimate=pl.CostEstimate(flops=0, bytes_accessed=300 << 20, transcendentals=0),
        name="exchange",
    )(lists, active_list, activations.reshape(BLOCKS, ROW_BLOCK, width))


def sums(table_ref, pool, weights, bias_ref, out_ref, slot):
    rows = pool.shape[1] * ROW_BLOCK
    unroll = 4

    def some(step, carry):
        for u in range(unroll):
            j = step * unroll + u
            taken = [pool[table_ref[j, k]].reshape(rows, TILE) for k in range(DEPTH)]
            panel = weights[table_ref[j, DEPTH], table_ref[j, DEPTH + 1]]
            total = jnp.dot(jnp.concatenate(taken, axis=1), panel, preferred_element_type=jnp.float32)
            total = jnp.clip(total + bias_ref[pl.ds(j, 1), :], 0.0, 32.0)
            at = pl.ds(pl.multiple_of(j * TILE, TILE), TILE)
            out_ref[pl.ds(slot * ROW_BLOCK, rows), at] = total.astype(jnp.bfloat16)
        return carry

    lax.fori_loop(0, PANELS // unroll, some, 0)


def levels(everyone_ref, unit):
    extra, room, extra_at, room_at = [], [], [jnp.int32(0)], [jnp.int32(0)]
    for v in range(UNIT):
        active = jnp.int32(0)
        for s in range(BLOCKS):
            active = active + jnp.where(everyone_ref[unit + v, s] < BLOCKS, 1, 0)
        extra.append(jnp.maximum(active - SHARED, 0))
        room.append(jnp.clip(SHARED - active, 0, SPARE))
        extra_at.append(extra_at[-1] + extra[-1])
        room_at.append(room_at[-1] + room[-1])
    return extra, room, extra_at, room_at


def hosted(everyone_ref, unit):
    extra, room, extra_at, room_at = levels(everyone_ref, unit.unit)
    mine, begin = jnp.int32(0), jnp.int32(0)
    for v in range(UNIT):
        mine = mine + jnp.where(unit.at == v, room[v], 0)
        begin = begin + jnp.where(unit.at == v, room_at[v], 0)
    guests = []
    for f in range(SPARE):
        turn = begin + f
        owner, which = jnp.int32(0), jnp.int32(0)
        for v in range(UNIT):
            hit = (turn >= extra_at[v]) & (turn < extra_at[v + 1])
            owner = owner + jnp.where(hit, v, 0)
            which = which + jnp.where(hit, turn - extra_at[v], 0)
        guests.append(((f < mine) & (turn < extra_at[UNIT]), owner, which))
    return guests


def layer_kernel(size, shared, lists_ref, everyone_ref, table_ref, pool_ref, spares_ref, panels_ref, bias_ref, *refs):
    groups = LATER[:-1] if shared else LATER
    count = len(groups)
    refs = list(refs)

    def take(n):
        part, refs[:n] = refs[:n], []
        return part

    ins, (out_ref,) = take(3 * count), take(1)
    returned_ref = take(1)[0] if shared else None
    pools, (pool, weights, send, recv, staged) = take(count), take(5)
    unit = Place() if shared else None
    lists = [ins[3 * n : 3 * n + 3] for n in range(count)]
    if shared:
        cast, mine, right, left, back_send, back_recv, cast_sem = refs
        given = lists[MIXED][0]
        lists[MIXED] = (mine, right, left)
        back = Spread(
            unit,
            out_ref.at[pl.ds(LATER[MIXED][0] * ROW_BLOCK, SPARE * ROW_BLOCK)],
            returned_ref,
            back_send,
            back_recv,
        )
    trades = [Trade(size, pools[n], lists[n][1], lists[n][2], send.at[n], recv.at[n]) for n in range(count)]
    barrier, met = greet(unit)
    loads = [
        pltpu.make_async_copy(panels_ref.at[:, pl.ds(n * DEPTH * TILE, DEPTH * TILE)], weights.at[n], staged.at[n])
        for n in range(weights.shape[0])
    ] + [pltpu.make_async_copy(pool_ref, pool, staged.at[2])]
    keeps = [
        pltpu.make_async_copy(lists[n][0], pools[n].at[pl.ds(OWN, HERE)], staged.at[3 + n]) for n in range(count)
    ]
    if shared:
        casting = [
            pltpu.make_async_copy(spares_ref, cast.at[pl.ds(0, UNIT)], cast_sem.at[0]),
            pltpu.make_async_copy(given, cast.at[UNIT], cast_sem.at[1]),
        ]
        for copy in casting:
            copy.start()
    pl.semaphore_wait(barrier, met)
    trades[0].heads()
    trades[0].tails()
    for n, copy in enumerate(keeps):
        if not (shared and n == MIXED):
            copy.start()
    if shared:
        guests = hosted(everyone_ref, unit)
        wait_all(casting)
        whose, which = [], []
        for i in range(SPARE):
            taken, owner, nth = guests[SPARE - 1 - i]
            whose.append(jnp.where(taken, owner, UNIT))
            which.append(jnp.where(taken, nth, i))

        def guest(s, carry):
            for i in range(SPARE):
                mine[s, i] = cast[whose[i], s, which[i]]
            return carry

        lax.fori_loop(0, HERE, guest, 0)
        pack(lists_ref, lambda block: mine[block], right, left, 0, size.listed)
        keeps[MIXED].start()
    trades[1].heads()
    trades[1].tails()
    for copy in loads:
        copy.start()
    trades[0].pass_on()
    wait_all(loads)
    sums(table_ref, pool, weights, bias_ref, out_ref, 0)
    trades[1].pass_on()
    for trade in trades[2:]:
        trade.heads()
        trade.tails()
    for n in [1, 0] + list(range(2, count)):
        trade = trades[n]
        keeps[n].wait()
        if n == 2:
            for other in trades[2:]:
                other.pass_on()
            if shared:
                back.relay()
        trade.finish()
        if shared and n == 2:
            back.relay_far()
        sums(table_ref, trade.pool, weights, bias_ref, out_ref, groups[n][0])
        if shared and n == MIXED:
            back.start()
    if shared:
        back.finish()


def layer(n, shared, lists, everyone, table, pool, spares, packed, panels, bias):
    size = SIZES[n]
    groups = LATER[:-1] if shared else LATER
    slots = SHARED if shared else BLOCKS
    width = PANELS * TILE
    outs = [jax.ShapeDtypeStruct((slots * ROW_BLOCK, width), jnp.bfloat16)]
    out_specs = [pl.BlockSpec(memory_space=pltpu.VMEM)]
    count = len(groups)
    scratch = [pltpu.VMEM((size.slots, m, ROW_BLOCK, TILE), jnp.bfloat16) for _, m in groups] + [
        pltpu.VMEM(pool.shape, jnp.bfloat16),
        pltpu.VMEM((2, panels.shape[0], DEPTH * TILE, TILE), jnp.bfloat16),
        pltpu.SemaphoreType.DMA((count, 6)),
        pltpu.SemaphoreType.DMA((count, 6)),
        pltpu.SemaphoreType.DMA((3 + count,)),
    ]
    if shared:
        outs.append(jax.ShapeDtypeStruct((UNIT, SPARE * ROW_BLOCK, width), jnp.bfloat16))
        out_specs.append(pl.BlockSpec(memory_space=pl.ANY))
        scratch += [pltpu.VMEM((UNIT + 1,) + spares.shape[1:], jnp.bfloat16)]
        scratch += [pltpu.VMEM(shape, jnp.bfloat16) for shape in packed_shapes(size, SPARE)]
        scratch += [
            pltpu.SemaphoreType.DMA((COPIES,)),
            pltpu.SemaphoreType.DMA((COPIES,)),
            pltpu.SemaphoreType.DMA((2,)),
        ]
    return pl.pallas_call(
        functools.partial(layer_kernel, size, shared),
        out_shape=outs,
        in_specs=[pl.BlockSpec(memory_space=pltpu.SMEM)] * 3
        + [pl.BlockSpec(memory_space=pl.ANY)] * 3
        + [pl.BlockSpec(memory_space=pltpu.VMEM)]
        + [pl.BlockSpec(memory_space=pl.ANY)] * (3 * count),
        out_specs=out_specs,
        scratch_shapes=scratch,
        compiler_params=pltpu.CompilerParams(
            collective_id=3 * n + (2 if shared else 1), has_side_effects=True, vmem_limit_bytes=62 << 20
        ),
        cost_estimate=pl.CostEstimate(flops=4 << 30, bytes_accessed=300 << 20, transcendentals=0),
        name="layer",
    )(lists, everyone, table, pool, spares, panels, bias, *packed[: 3 * count])


def place_kernel(shared, row_ref, everyone_ref, *refs):
    out_ref, returned_ref = refs[0], refs[1] if shared else None
    result_ref, stage, read, write = refs[-4:]
    row = row_ref[0]
    unit = (row // UNIT) * UNIT
    held = SHARED if shared else BLOCKS
    slots = []
    for b in range(BLOCKS):
        slot = jnp.int32(-1)
        for s in range(BLOCKS):
            slot = jnp.where(everyone_ref[row, s] == b, s, slot)
        slots.append(slot)

        @pl.when((slot >= 0) & (slot < held))
        def _():
            at = pl.multiple_of(slot * ROW_BLOCK, ROW_BLOCK)
            pltpu.make_async_copy(out_ref.at[pl.ds(at, ROW_BLOCK)], stage.at[b], read.at[b]).start()

    if shared:
        extra, room, extra_at, room_at = levels(everyone_ref, unit)
        begin = jnp.int32(0)
        for v in range(UNIT):
            begin = begin + jnp.where(row - unit == v, extra_at[v], 0)
        for b in range(BLOCKS):

            @pl.when(slots[b] >= held)
            def _():
                turn = begin + slots[b] - SHARED
                host, nth = jnp.int32(0), jnp.int32(0)
                for v in range(UNIT):
                    hit = (turn >= room_at[v]) & (turn < room_at[v + 1])
                    host = host + jnp.where(hit, v, 0)
                    nth = nth + jnp.where(hit, turn - room_at[v], 0)
                at = pl.multiple_of((SPARE - 1 - nth) * ROW_BLOCK, ROW_BLOCK)
                pltpu.make_async_copy(returned_ref.at[host, pl.ds(at, ROW_BLOCK)], stage.at[b], read.at[b]).start()

    writes = []
    for b in range(BLOCKS):

        @pl.when(slots[b] < 0)
        def _():
            stage[b] = jnp.zeros(stage.shape[1:], stage.dtype)

        @pl.when(slots[b] >= 0)
        def _():
            pltpu.make_async_copy(out_ref.at[pl.ds(0, ROW_BLOCK)], stage.at[b], read.at[b]).wait()

        to = result_ref.at[pl.ds(b * ROW_BLOCK, ROW_BLOCK)]
        writes.append(pltpu.make_async_copy(stage.at[b], to, write.at[b]))
        writes[-1].start()
    wait_all(writes)


def place(shared, everyone, outs):
    row = lax.axis_index("rows").astype(jnp.int32).reshape(1)
    width = outs[0].shape[1]
    return pl.pallas_call(
        functools.partial(place_kernel, shared),
        out_shape=jax.ShapeDtypeStruct((BLOCKS * ROW_BLOCK, width), jnp.bfloat16),
        in_specs=[pl.BlockSpec(memory_space=pltpu.SMEM)] * 2 + [pl.BlockSpec(memory_space=pl.ANY)] * len(outs),
        out_specs=pl.BlockSpec(memory_space=pl.ANY),
        scratch_shapes=[
            pltpu.VMEM((BLOCKS, ROW_BLOCK, width), jnp.bfloat16),
            pltpu.SemaphoreType.DMA((BLOCKS,)),
            pltpu.SemaphoreType.DMA((BLOCKS,)),
        ],
        compiler_params=pltpu.CompilerParams(vmem_limit_bytes=62 << 20),
        name="place",
    )(row, everyone, *outs)


def general(activations, weight_tiles, panel_map, block_index, active_list, bias):
    row_count, local_width = activations.shape
    blocks_here = row_count // ROW_BLOCK
    listed = active_list[0]
    picked = jnp.minimum(listed, blocks_here - 1)
    gathered = lax.all_gather(activations, "cols", axis=1, tiled=True)
    compact = jnp.take(gathered.reshape(blocks_here, ROW_BLOCK, -1), picked, axis=0)
    slot_rows = compact.shape[0] * ROW_BLOCK
    tile_view = compact.reshape(slot_rows, -1, TILE)
    panels_here = panel_map.shape[1]
    columns = lax.axis_index("cols") * panels_here + panel_map[0]
    sources = jnp.take(block_index, columns, axis=0)
    panel_block = lax.all_gather(weight_tiles[0], "rows", axis=0, tiled=True)
    count_here = panel_block.shape[0]
    total = jnp.zeros((slot_rows, count_here, TILE), jnp.float32)
    for depth in range(panel_block.shape[1]):
        chosen = jnp.take(tile_view, sources[:, depth], axis=1)
        total = total + jnp.einsum(
            "mpt,pts->mps", chosen, panel_block[:, depth], preferred_element_type=jnp.float32
        )
    ordered = jnp.take(total, jnp.argsort(panel_map[0]), axis=1).reshape(slot_rows, -1)
    clamped = jnp.minimum(jnp.maximum(ordered + bias[None, :], 0.0), 32.0).astype(jnp.bfloat16)
    placing = (listed[:, None] == jnp.arange(blocks_here, dtype=jnp.int32)[None, :]).astype(
        jnp.bfloat16
    )
    spread = jnp.einsum(
        "sb,srw->brw",
        placing,
        clamped.reshape(listed.shape[0], ROW_BLOCK, -1),
        preferred_element_type=jnp.float32,
    )
    return spread.astype(jnp.bfloat16).reshape(row_count, -1)


def body(activations, weight_tiles, panel_map, block_index, active_list, bias):
    at = lax.axis_index("cols").astype(jnp.int32).reshape(1)
    lists, choice, *tables, held = plan(at, active_list, block_index, panel_map, weight_tiles.reshape(-1, TILE))

    def sparse(n):
        def branch(lists, tables, held, activations, weight_tiles, panel_map, block_index, active_list, bias):
            panels = lax.all_gather(held, "rows", axis=0, tiled=False)
            pool, spares, *packed = exchange(n, lists, active_list, activations)
            everyone = panels[:, held.shape[0] - ROW_BLOCK, :BLOCKS].astype(jnp.int32)
            active = jnp.sum(everyone < BLOCKS, axis=1, dtype=jnp.int32).reshape(-1, UNIT)
            left_over = jnp.maximum(active - SHARED, 0) - jnp.clip(SHARED - active, 0, SPARE)
            level = jnp.all(jnp.sum(left_over, axis=1) <= 0)
            biases = bias.reshape(PANELS, TILE)

            def finish(shared):
                def last(lists, everyone, table, pool, spares, packed, panels, biases):
                    outs = layer(n, shared, lists, everyone, table, pool, spares, packed, panels, biases)
                    return place(shared, everyone, outs)

                return last

            return lax.cond(
                level, finish(True), finish(False), lists, everyone, tables[n], pool, spares, packed, panels, biases
            )

        return branch

    def dense(lists, tables, held, *rest):
        return general(*rest)

    branches = [sparse(n) for n in range(len(SIZES))] + [dense]
    rest = (activations, weight_tiles, panel_map, block_index, active_list, bias)
    return lax.switch(choice[0], branches, lists, tables, held, *rest)


def solution(mesh):
    in_specs = (
        P("rows", "cols"),
        P("cols", "rows", None, None, None),
        P("cols", None),
        P(),
        P("rows", None),
        P("cols"),
    )
    out_specs = P("rows", "cols")
    return jax.shard_map(body, mesh=mesh, in_specs=in_specs, out_specs=out_specs, check_vma=False)
```
